256 devices in a mesh: gx: 16 (over z_hi, x), gy: 16 (over z_lo, y, core).
Axes of the slice: x: 4, y: 4, z: 8 (z_hi: 4, z_lo: 2; z = z_hi * 2 + z_lo), core: 2. Of those that a mesh axis runs over, the one named last changes fastest.
Arguments:
- positions: float32 [3, 32, 32, 128], P(None, 'gx', 'gy'), may hold values from 0 to 192, as said below
- valid_mask: int32 [32, 32, 128], P('gx', 'gy'), may hold values from 0 to 1, as said below
- species: int32 [32, 32, 128], P('gx', 'gy'), may hold values from 0 to 3
- density_table: float32 [32, 256], replicated, may hold values from -1 to 1
- radial_gain: float32 [8, 256], replicated, may hold values from -4 to 4
- readout: bfloat16 [256, 16], replicated, may hold values from -0.375 to 0.375
Outputs:
- forces: float32 [3, 32, 32, 128], P(None, 'gx', 'gy')
- energies: float32 [16, 32, 32, 128], P(None, 'gx', 'gy')
The draws below stay inside these ranges and needn't reach their ends.
Inputs may be any that keep to these rules, and one draw needn't show every extreme that they name: `positions`: the atoms of cell (a, b) lie at x in [6 a, 6 a + 6), y in [6 b, 6 b + 6) and z in [0, 0.3 * 128). `valid_mask`: in each cell the slots holding 1 come before those holding 0.
All inputs are finite; a program needn't handle non-finite values.
Results may differ from the reference program's by a relative error of at most 0.0095.
Values sent between devices are 32-bit elements; how exact they have to be, the bound alone decides.
A program may use at most 128 MiB of HBM per device.

```python
import jax
import jax.numpy as jnp
from jax import lax

ATOMS_CELL = 128
CHANNELS = 256
RADIAL = 8
SPECIES = 4
HEADS = 16
NX = 32
NY = 32


def draw_positions(key, part):
    key = jax.random.fold_in(key, 7)
    key_plane, key_height = jax.random.split(key, 2)
    plane = jax.random.uniform(key_plane, (2, NX, NY, ATOMS_CELL), jnp.float32)
    height = jax.random.uniform(key_height, (NX, NY, ATOMS_CELL), jnp.float32)
    column_x = jnp.arange(NX, dtype=jnp.float32)[:, None, None]
    column_y = jnp.arange(NY, dtype=jnp.float32)[None, :, None]
    coord_x = (column_x + plane[0]) * 6.0
    coord_y = (column_y + plane[1]) * 6.0
    coord_z = height * (0.3 * ATOMS_CELL)
    return jnp.stack([coord_x, coord_y, coord_z], 0).astype(jnp.float32)


def draw_valid_mask(key, part):
    key = jax.random.fold_in(key, 11)
    key_empty, key_count = jax.random.split(key, 2)
    column_x = jnp.arange(NX, dtype=jnp.int32)[:, None]
    empty = jax.random.randint(key_empty, (NX, NY), 0, NX, dtype=jnp.int32) < column_x
    filled = jax.random.randint(key_count, (NX, NY), ATOMS_CELL // 2, ATOMS_CELL + 1, dtype=jnp.int32)
    counts = jnp.where(empty, 0, filled)
    slots = jnp.arange(ATOMS_CELL, dtype=jnp.int32)[None, None, :]
    return (slots < counts[:, :, None]).astype(jnp.int32)


def with_ends(array, key, low, high):
    longest = array.shape.index(max(array.shape))
    spots = []
    for shift in (0, 1):
        where = [jax.random.randint(jax.random.fold_in(key, axis), (), 0, length) for axis, length in enumerate(array.shape)]
        where[longest] = (where[longest] + shift) % array.shape[longest]
        spots.append(tuple(where))
    return array.at[spots[0]].set(low).at[spots[1]].set(high)


def scatter_about(stream_key, shape, scale, most, kind=jnp.bfloat16):
    return jnp.clip(scale * jax.random.normal(stream_key, shape, jnp.float32), -most, most).astype(kind)


def setup_inputs(seed: int = 0) -> dict:
    key_list = jax.random.split(jax.random.key(seed), 7)
    return {
        "positions": draw_positions(jax.random.fold_in(key_list[6], 71), 0),
        "valid_mask": draw_valid_mask(jax.random.fold_in(key_list[6], 71), 0),
        "species": with_ends(jax.random.randint(key_list[2], (NX, NY, ATOMS_CELL), 0, SPECIES), jax.random.fold_in(key_list[2], 1), 0, SPECIES - 1).astype(jnp.int32),
        "density_table": scatter_about(key_list[3], (RADIAL * SPECIES, CHANNELS), (RADIAL * SPECIES) ** -0.5, 1.0, jnp.float32),
        "radial_gain": scatter_about(key_list[4], (RADIAL, CHANNELS), 1.0, 4.0, jnp.float32),
        "readout": scatter_about(key_list[5], (CHANNELS, HEADS), CHANNELS ** -0.5, 0.375),
    }


cutoff_radius = 6.0
soften_sq = 0.01
norm_one = 8.0
norm_two = 32.0

def pair_basis(near_pos, near_valid):
    count = near_pos.shape[-1]
    own_pos = near_pos[:, 1, 1, :]
    own_valid = near_valid[1, 1, :]
    flat_pos = near_pos.reshape(3, 9, count)
    flat_valid = near_valid.reshape(9, count)
    offset = own_pos[:, :, None, None] - flat_pos[:, None, :, :]
    distance = jnp.sqrt(lax.optimization_barrier(jnp.sum(offset * offset, axis=0)) + soften_sq)
    reach = jnp.maximum(1.0 - jnp.square(distance / cutoff_radius), 0.0)
    atom_ids = jnp.arange(count, dtype=jnp.int32)
    cell_ids = jnp.arange(9, dtype=jnp.int32)
    self_pair = (atom_ids[:, None, None] == atom_ids[None, None, :]) & (cell_ids[None, :, None] == 4)
    weight = own_valid[:, None, None] * flat_valid[None, :, :] * jnp.where(self_pair, 0.0, 1.0) * reach * reach
    spacing = cutoff_radius / (RADIAL - 1)
    centres = jnp.arange(RADIAL, dtype=jnp.float32) * spacing
    gaussian = jnp.exp(-jnp.square((distance[:, :, None, :] - centres[None, None, :, None]) / spacing))
    return weight[:, :, None, :] * gaussian

def density_block(near_pos, near_valid, near_species):
    count = near_pos.shape[-1]
    radial_basis = pair_basis(near_pos, near_valid)
    kinds = jnp.arange(SPECIES, dtype=jnp.float32)
    onehot = (near_species.reshape(9, count)[:, :, None] == kinds[None, None, :]).astype(jnp.float32)
    density = jnp.einsum('icku,cus->iks', radial_basis, onehot, precision=lax.Precision.HIGHEST)
    return density.reshape(count, RADIAL * SPECIES)

def cell_densities(pos_padded, valid_padded, species_padded):
    span_x = pos_padded.shape[1] - 2
    span_y = pos_padded.shape[2] - 2
    count = pos_padded.shape[3]

    def one_cell(cell_index):
        zero = jnp.zeros((), jnp.int32)
        row_index = (cell_index // span_y).astype(jnp.int32)
        col_index = (cell_index % span_y).astype(jnp.int32)
        near_pos = lax.dynamic_slice(pos_padded, (zero, row_index, col_index, zero), (3, 3, 3, count))
        near_valid = lax.dynamic_slice(valid_padded, (row_index, col_index, zero), (3, 3, count))
        near_species = lax.dynamic_slice(species_padded, (row_index, col_index, zero), (3, 3, count))
        return density_block(near_pos, near_valid, near_species)
    density = lax.map(jax.checkpoint(one_cell), jnp.arange(span_x * span_y, dtype=jnp.int32))
    return density.reshape(span_x, span_y, count, RADIAL * SPECIES)

def activate(density, density_table):
    product = jnp.dot(density, density_table, precision=lax.Precision.HIGHEST, preferred_element_type=jnp.float32)
    return jax.nn.silu(product / norm_one)

def cell_energy(near_pos, near_hidden, near_valid, radial_gain, readout):
    count = near_pos.shape[-1]
    width = near_hidden.shape[-1]
    radial_basis = pair_basis(near_pos, near_valid).astype(jnp.bfloat16).reshape(count, 9 * RADIAL * count)
    scaled = (near_hidden.reshape(9, 1, count, width) * radial_gain[None, :, None, :]).astype(jnp.bfloat16)
    scaled = scaled.reshape(9 * RADIAL * count, width)
    message = jnp.dot(radial_basis, scaled, preferred_element_type=jnp.float32)
    hidden_two = jax.nn.silu(message / norm_two + near_hidden[1, 1]).astype(jnp.bfloat16)
    head_input = jnp.dot(hidden_two, readout, preferred_element_type=jnp.float32)
    return (near_valid[1, 1][:, None] * jax.nn.silu(head_input)).T

def layer_two(pos_padded, hidden_padded, valid_padded, radial_gain, readout):
    span_x = pos_padded.shape[1] - 2
    span_y = pos_padded.shape[2] - 2
    count = pos_padded.shape[3]
    width = hidden_padded.shape[3]

    def one_cell(cell_index):
        zero = jnp.zeros((), jnp.int32)
        row_index = (cell_index // span_y).astype(jnp.int32)
        col_index = (cell_index % span_y).astype(jnp.int32)
        near_pos = lax.dynamic_slice(pos_padded, (zero, row_index, col_index, zero), (3, 3, 3, count))
        near_hidden = lax.dynamic_slice(hidden_padded, (row_index, col_index, zero, zero), (3, 3, count, width))
        near_valid = lax.dynamic_slice(valid_padded, (row_index, col_index, zero), (3, 3, count))
        return cell_energy(near_pos, near_hidden, near_valid, radial_gain, readout)
    return lax.map(jax.checkpoint(one_cell), jnp.arange(span_x * span_y, dtype=jnp.int32))

def reference(positions, valid_mask, species, density_table, radial_gain, readout):
    valid_float = valid_mask.astype(jnp.float32)
    species_float = species.astype(jnp.float32)
    valid_padded = jnp.pad(valid_float, ((1, 1), (1, 1), (0, 0)))
    species_padded = jnp.pad(species_float, ((1, 1), (1, 1), (0, 0)))

    def evaluate(coords):
        pos_padded = jnp.pad(coords, ((0, 0), (1, 1), (1, 1), (0, 0)))
        density = cell_densities(pos_padded, valid_padded, species_padded)
        hidden = activate(density, density_table)
        hidden_padded = jnp.pad(hidden, ((1, 1), (1, 1), (0, 0), (0, 0)))
        energy = layer_two(pos_padded, hidden_padded, valid_padded, radial_gain, readout)
        return (jnp.sum(energy) / energy.shape[1], energy)
    (energy_sum, energy), gradient = jax.value_and_grad(evaluate, has_aux=True)(positions)
    energies = energy.reshape(NX, NY, energy.shape[1], energy.shape[2]).transpose(2, 0, 1, 3)
    return (-gradient, energies)
```

```python
import functools
import math

import jax
import jax.numpy as jnp
from jax import lax
from jax.experimental import pallas as pl
from jax.experimental.pallas import tpu as pltpu
from jax.sharding import PartitionSpec as P

MESH = pl.DeviceIdType.MESH
F32 = jnp.float32
BF16 = jnp.bfloat16

RADIAL = 8
SPECIES = 4
N = 128
CH = 256
CUT = 6.0
SOFT = 0.01
SPACE = CUT / (RADIAL - 1)
COEF = [math.exp(8.0 * k - k * k) for k in range(RADIAL)]
DIRS = [(dx, dy) for dx in (-1, 0, 1) for dy in (-1, 0, 1) if (dx, dy) != (0, 0)]
OWN = 4 * N
HALO = 5 * N
ROWS = 32
BLOCKS = N // ROWS


def nn(a, b):
    return lax.dot_general(a, b, (((1,), (0,)), ((), ())), preferred_element_type=F32)


def nt(a, b):
    return lax.dot_general(a, b, (((1,), (1,)), ((), ())), preferred_element_type=F32)


def border(d):
    return {1: 2, -1: 1, 0: pl.ds(1, 2)}[d]


def landing(d):
    return {1: 0, -1: 3, 0: pl.ds(1, 2)}[d]


def beyond(d):
    return {1: 3, -1: 0, 0: pl.ds(1, 2)}[d]


def own_slot(c):
    return 1 + c // 2, 1 + c % 2


def halo_slots(c):
    a_out, b_out = 3 * (c // 2), 3 * (c % 2)
    return [(a_out, b_out), (a_out, 1), (a_out, 2), (1, b_out), (2, b_out)]


def sigmoid(x):
    return 1.0 / (1.0 + jnp.exp(-x))


def kernel(
    nx, ny,
    pos_ref, valid_ref, spec_ref, table_ref, gain_ref, readout_ref,
    forces_ref, energies_ref,
    atoms, xi, basis, u_s, a_s, rc_s, ri_s, dens, hid_t, hid, hid_own, slope,
    msg, gms, gms_t, gm_t, g1, onehot, tab_t, tab_s, gk, gk_t, read_t,
    gpart, grecv, gsum, fi, fj, fpart, frecv, gs,
    send_sem, recv_sem,
):
    gx, gy = lax.axis_index("gx"), lax.axis_index("gy")

    def there(dx, dy):
        ok = None
        for d, g, n in ((dx, gx, nx), (dy, gy, ny)):
            if d:
                one = (g < n - 1) if d > 0 else (g > 0)
                ok = one if ok is None else jnp.logical_and(ok, one)
        return ok

    def copy(r, n, src, dst, peer):
        return pltpu.make_async_remote_copy(
            src_ref=src, dst_ref=dst, send_sem=send_sem.at[r, n], recv_sem=recv_sem.at[r, n],
            device_id=peer, device_id_type=MESH,
        )

    def outward(r, buf, wait):
        for n, (dx, dy) in enumerate(DIRS):
            src = buf.at[border(dx), border(dy)]
            dst = buf.at[landing(dx), landing(dy)]
            if wait == "recv":
                @pl.when(there(-dx, -dy))
                def _():
                    copy(r, n, src, dst, (gx - dx, gy - dy)).wait_recv()
            else:
                @pl.when(there(dx, dy))
                def _():
                    c = copy(r, n, src, dst, (gx + dx, gy + dy))
                    c.start() if wait == "start" else c.wait_send()

    def inward(r, buf, land, wait):
        for n, (dx, dy) in enumerate(DIRS):
            src = buf.at[beyond(dx), beyond(dy)]
            dst = land.at[n, 0] if dx and dy else land.at[n]
            if wait == "recv":
                @pl.when(there(-dx, -dy))
                def _():
                    copy(r, n, src, dst, (gx - dx, gy - dy)).wait_recv()
            else:
                @pl.when(there(dx, dy))
                def _():
                    c = copy(r, n, src, dst, (gx + dx, gy + dy))
                    c.start() if wait == "start" else c.wait_send()

    def returned(land, a, b):
        total = None
        for n, (dx, dy) in enumerate(DIRS):
            if (dx == 0 or a == (1 if dx == 1 else 2)) and (dy == 0 or b == (1 if dy == 1 else 2)):
                m = a - 1 if dx == 0 else (b - 1 if dy == 0 else 0)
                total = land[n, m] if total is None else total + land[n, m]
        return total

    for a in range(4):
        for b in range(4):
            if a in (1, 2) and b in (1, 2):
                rows = [pos_ref[i, a - 1, b - 1 : b, :] for i in range(3)]
                rows.append(valid_ref[a - 1, b - 1 : b, :].astype(F32))
                rows.append(spec_ref[a - 1, b - 1 : b, :].astype(F32))
                rows.append(jnp.zeros((3, N), F32))
                atoms[a, b] = jnp.concatenate(rows, 0)
            else:
                atoms[a, b] = jnp.zeros((8, N), F32)
                dens[a, b] = jnp.zeros((RADIAL * SPECIES, N), F32)
    grecv[...] = jnp.zeros_like(grecv)
    frecv[...] = jnp.zeros_like(frecv)

    barrier = pltpu.get_barrier_semaphore()
    for dx, dy in DIRS:
        @pl.when(there(dx, dy))
        def _():
            pl.semaphore_signal(barrier, inc=1, device_id=(gx + dx, gy + dy), device_id_type=MESH)
    span_x = 1 + jnp.where(gx > 0, 1, 0) + jnp.where(gx < nx - 1, 1, 0)
    span_y = 1 + jnp.where(gy > 0, 1, 0) + jnp.where(gy < ny - 1, 1, 0)

    table = table_ref[...] * 0.125
    high = table.astype(BF16).astype(F32)
    low = table - high
    tab_s[...] = jnp.concatenate([high, low], 0).astype(BF16)
    stacked = jnp.concatenate([high, high, low, jnp.zeros((32, CH), F32)], 0)
    tab_t[...] = stacked.T.astype(BF16)
    for k in range(RADIAL):
        row = gain_ref[k : k + 1, :] * (COEF[k] / 32.0)
        gk[k] = row
        gk_t[k] = jnp.broadcast_to(row, (N, CH)).T
    readout_f = jnp.concatenate([readout_ref[...].astype(F32), jnp.zeros((CH, N - 16), F32)], 1)
    read_t[...] = readout_f.T.astype(BF16)
    for c in range(4):
        a, b = own_slot(c)
        tile = atoms[a, b]
        x = jnp.where(tile[3:4] > 0.0, tile[0:1], 1e4)
        xi[c, 0] = jnp.broadcast_to(x, (N, N)).T
        xi[c, 1] = jnp.broadcast_to(tile[1:2], (N, N)).T
        xi[c, 2] = jnp.broadcast_to(tile[2:3], (N, N)).T

    pl.semaphore_wait(barrier, span_x * span_y - 1)
    outward(0, atoms, "start")

    def offsets(c, rows, a, b):
        xj = jnp.where(atoms[a, b, 3:4, :] > 0.0, atoms[a, b, 0:1, :], -1e4)
        dx = xi[c, 0, rows, :] - xj
        dy = xi[c, 1, rows, :] - atoms[a, b, 1:2, :]
        dz = xi[c, 2, rows, :] - atoms[a, b, 2:3, :]
        return dx, dy, dz

    def pair_basis(c, block, a, b, lane, self_cell):
        rows = pl.ds(block * ROWS, ROWS)
        cols = slice(lane, lane + N)
        dx, dy, dz = offsets(c, rows, a, b)
        sq = dx * dx + dy * dy + (dz * dz + SOFT)
        if self_cell is not None:
            i = lax.broadcasted_iota(jnp.int32, (ROWS, N), 0) + block * ROWS
            j = lax.broadcasted_iota(jnp.int32, (ROWS, N), 1)
            sq = jnp.where(jnp.logical_and(i == j, self_cell), 1e8, sq)
        ri = lax.rsqrt(sq)
        reach = jnp.maximum(1.0 - sq * (1.0 / (CUT * CUT)), 0.0)
        t = jnp.minimum(sq * ri * (1.0 / SPACE), float(RADIAL - 1))
        u = jnp.exp(2.0 * t - 8.0)
        amp = jnp.exp(-(t * t)) * reach
        u_s[c, rows, cols] = u
        a_s[c, rows, cols] = amp
        rc_s[c, rows, cols] = reach
        ri_s[c, rows, cols] = ri
        term = amp * reach
        for k in range(RADIAL):
            basis[c, pl.ds(k * N + block * ROWS, ROWS), cols] = term.astype(BF16)
            if k < RADIAL - 1:
                term = term * u

    def own_pairs(step, carry):
        c, block = step // BLOCKS, step % BLOCKS
        for j in range(4):
            a, b = own_slot(j)
            pair_basis(c, block, a, b, j * N, c == j)
        return carry

    def halo_pairs(step, carry):
        c, block = step // BLOCKS, step % BLOCKS
        for m, (a, b) in enumerate(halo_slots(c)):
            pair_basis(c, block, a, b, OWN + m * N, None)
        return carry

    lax.fori_loop(0, 4 * BLOCKS, own_pairs, 0)
    outward(0, atoms, "recv")
    for a in range(4):
        for b in range(4):
            kind = atoms[a, b, 4:5, :].astype(jnp.int32)
            r = lax.broadcasted_iota(jnp.int32, (N, N), 0)
            hit = jnp.logical_and(r < 64, (r & 3) == kind)
            onehot[a, b] = jnp.where(hit, 1.0, 0.0).astype(BF16)
    lax.fori_loop(0, 4 * BLOCKS, halo_pairs, 0)

    def kinds(a, b):
        kind = atoms[a, b, 4:5, :].astype(jnp.int32)
        r = lax.broadcasted_iota(jnp.int32, (16, N), 0)
        return jnp.where(r == kind, 1.0, 0.0).astype(BF16)

    def densities(c, carry):
        cells = [own_slot(j) for j in range(4)] + halo_slots(c)
        hot = jnp.concatenate([kinds(a, b) for a, b in cells], 1)
        out = nt(hot, basis[c])
        a, b = own_slot(c)
        for k in range(RADIAL):
            dens[a, b, k * SPECIES : (k + 1) * SPECIES, :] = (
                out[0:SPECIES, k * N : (k + 1) * N] * COEF[k]
            )
        return carry

    lax.fori_loop(0, 4, densities, 0)
    outward(1, dens, "start")

    def features(a, b):
        d = dens[a, b]
        top = d.astype(BF16)
        rest = (d - top.astype(F32)).astype(BF16)
        cat = jnp.concatenate([top, rest, top, jnp.zeros((32, N), BF16)], 0)
        z = nn(tab_t[...], cat)
        s = sigmoid(z)
        h = z * s
        hid_t[a, b] = h.astype(BF16)
        slope[a, b] = s * (1.0 + z * (1.0 - s))
        return h.T

    def own_features(c, carry):
        a, b = own_slot(c)
        h = features(a, b)
        hid_own[c] = h
        hid[a, b] = h.astype(BF16)
        return carry

    lax.fori_loop(0, 4, own_features, 0)

    def gained(prod):
        total = prod[0:N] * gk[0]
        for k in range(1, RADIAL):
            total = total + prod[k * N : (k + 1) * N] * gk[k]
        return total

    def own_message(c, carry):
        h = jnp.concatenate([hid[a, b] for a, b in [own_slot(j) for j in range(4)]], 0)
        msg[c] = gained(nn(basis[c, :, 0:OWN], h))
        return carry

    lax.fori_loop(0, 4, own_message, 0)
    outward(1, dens, "recv")

    def halo_features(step, carry):
        q = step - 8
        a = jnp.where(step < 8, 3 * (step // 4), 1 + q // 2)
        b = jnp.where(step < 8, step % 4, 3 * (q % 2))
        hid[a, b] = features(a, b).astype(BF16)
        return carry

    lax.fori_loop(0, 12, halo_features, 0)

    def second_layer(c, carry):
        a, b = own_slot(c)
        h = jnp.concatenate([hid[p, q] for p, q in halo_slots(c)], 0)
        m = msg[c] + gained(nn(basis[c, :, OWN:], h))
        p = m + hid_own[c]
        s = sigmoid(p)
        second = (p * s).astype(BF16)
        heads = nt(read_t[...], second)
        valid = atoms[a, b, 3:4, :]
        sh = sigmoid(heads)
        energies_ref[a - 1, b - 1] = (valid * (heads * sh))[0:16]
        back = (valid * (1.0 / 16.0)) * (sh * (1.0 + heads * (1.0 - sh)))
        dsec = nn(back.T.astype(BF16), read_t[...]).astype(BF16).astype(F32)
        gm = dsec * (s * (1.0 + p * (1.0 - s)))
        gmt = gm.T
        gm_t[c] = gmt
        for k in range(RADIAL):
            gms[c, k * N : (k + 1) * N, :] = (gm * gk[k]).astype(BF16)
            gms_t[c, :, k * N : (k + 1) * N] = (gmt * gk_t[k]).astype(BF16)
        return carry

    lax.fori_loop(0, 4, second_layer, 0)

    gpart[...] = jnp.zeros_like(gpart)

    def project(x):
        out = nn(tab_s[...], x.astype(BF16))
        return out[0:32] + out[32:64]

    def halo_grad(c, carry):
        x = nn(gms_t[c], basis[c, :, OWN:])
        for m, (a, b) in enumerate(halo_slots(c)):
            gpart[a, b] += project(x[:, m * N : (m + 1) * N] * slope[a, b])
        return carry

    lax.fori_loop(0, 4, halo_grad, 0)
    inward(2, gpart, grecv, "start")

    def own_grad(j, carry):
        a, b = own_slot(j)
        cols = pl.ds(pl.multiple_of(j * N, N), N)
        x = gm_t[j]
        for c in range(4):
            x = x + nn(gms_t[c], basis[c, :, cols])
        gsum[j] = project(x * slope[a, b])
        return carry

    lax.fori_loop(0, 4, own_grad, 0)
    inward(2, gpart, grecv, "recv")

    for c in range(4):
        a, b = own_slot(c)
        g = gsum[c] + returned(grecv, a, b)
        r = lax.broadcasted_iota(jnp.int32, (32, N), 0) >> 2
        coef = jnp.full((32, N), COEF[0], F32)
        for k in range(1, RADIAL):
            coef = jnp.where(r == k, COEF[k], coef)
        g = g * coef
        top = g.astype(BF16).astype(F32)
        gt = jnp.concatenate([top, g - top, jnp.zeros((64, N), F32)], 0).T
        lane = lax.broadcasted_iota(jnp.int32, (N, N), 1)
        for k in range(RADIAL):
            keep = jnp.logical_and(lane < 64, ((lane & 31) >> 2) == k)
            g1[c, k * N : (k + 1) * N, :] = jnp.where(keep, gt, 0.0).astype(BF16)

    fi[...] = jnp.zeros_like(fi)
    fj[...] = jnp.zeros_like(fj)

    def pair_forces(c, cells, lane0):
        h = jnp.concatenate([hid_t[a, b] for a, b in cells], 1)
        o = jnp.concatenate([onehot[a, b] for a, b in cells], 1)
        width = len(cells) * N
        gs[:, 0:width] = nn(gms[c], h) + nn(g1[c], o)

        def body(block, carry):
            rows = pl.ds(block * ROWS, ROWS)
            sums = [jnp.zeros((ROWS, N), F32) for _ in range(3)]
            for m, (a, b) in enumerate(cells):
                cols = slice(lane0 + m * N, lane0 + (m + 1) * N)
                u = u_s[c, rows, cols]

                def grad(k):
                    return gs[pl.ds(k * N + block * ROWS, ROWS), m * N : (m + 1) * N]

                poly = grad(RADIAL - 1)
                slant = poly
                for k in range(RADIAL - 2, -1, -1):
                    poly = poly * u + grad(k)
                    if k:
                        slant = slant * u + poly
                slant = slant * u
                reach = rc_s[c, rows, cols]
                inner = ri_s[c, rows, cols] * slant * (2.0 / SPACE) - poly * (2.0 / SPACE**2)
                force = a_s[c, rows, cols] * (reach * inner - poly * (4.0 / CUT**2))
                for i, d in enumerate(offsets(c, rows, a, b)):
                    f = force * d
                    sums[i] = sums[i] + f
                    part = f[0:8]
                    for q in range(1, ROWS // 8):
                        part = part + f[8 * q : 8 * q + 8]
                    fj[a, b, i] += part
            for i in range(3):
                fi[c, i, rows, :] += sums[i]
            return carry

        lax.fori_loop(0, BLOCKS, body, 0)

    def halo_forces(c, carry):
        pair_forces(c, halo_slots(c), OWN)
        return carry

    def own_forces(c, carry):
        pair_forces(c, [own_slot(j) for j in range(4)], 0)
        return carry

    lax.fori_loop(0, 4, halo_forces, 0)
    for a in range(4):
        for b in range(4):
            if not (a in (1, 2) and b in (1, 2)):
                rows = [jnp.sum(fj[a, b, i], 0, keepdims=True) for i in range(3)]
                fpart[a, b] = jnp.concatenate(rows + [jnp.zeros((5, N), F32)], 0)
    inward(3, fpart, frecv, "start")
    lax.fori_loop(0, 4, own_forces, 0)
    sums = []
    for c in range(4):
        a, b = own_slot(c)
        rows = []
        for i in range(3):
            mine = jnp.sum(fi[c, i].T, 0, keepdims=True)
            rows.append(jnp.sum(fj[a, b, i], 0, keepdims=True) - mine)
        sums.append(jnp.concatenate(rows + [jnp.zeros((5, N), F32)], 0))
    inward(3, fpart, frecv, "recv")
    for c in range(4):
        a, b = own_slot(c)
        forces_ref[a - 1, b - 1] = sums[c] + returned(frecv, a, b)
    outward(0, atoms, "send")
    outward(1, dens, "send")
    inward(2, gpart, grecv, "send")
    inward(3, fpart, frecv, "send")


def shards(nx, ny, positions, valid_mask, species, density_table, radial_gain, readout):
    vmem = pltpu.VMEM
    whole = pl.BlockSpec(memory_space=pltpu.VMEM)
    wide = OWN + HALO
    forces, energies = pl.pallas_call(
        functools.partial(kernel, nx, ny),
        out_shape=(
            jax.ShapeDtypeStruct((2, 2, 8, N), F32),
            jax.ShapeDtypeStruct((2, 2, 16, N), F32),
        ),
        in_specs=[whole] * 6,
        out_specs=(whole, whole),
        scratch_shapes=[
            vmem((4, 4, 8, N), F32),
            vmem((4, 3, N, N), F32),
            vmem((4, RADIAL * N, wide), BF16),
            vmem((4, N, wide), F32),
            vmem((4, N, wide), F32),
            vmem((4, N, wide), F32),
            vmem((4, N, wide), F32),
            vmem((4, 4, RADIAL * SPECIES, N), F32),
            vmem((4, 4, CH, N), BF16),
            vmem((4, 4, N, CH), BF16),
            vmem((4, N, CH), F32),
            vmem((4, 4, CH, N), F32),
            vmem((4, N, CH), F32),
            vmem((4, RADIAL * N, CH), BF16),
            vmem((4, CH, RADIAL * N), BF16),
            vmem((4, CH, N), F32),
            vmem((4, RADIAL * N, N), BF16),
            vmem((4, 4, N, N), BF16),
            vmem((CH, N), BF16),
            vmem((64, CH), BF16),
            vmem((RADIAL, 1, CH), F32),
            vmem((RADIAL, CH, N), F32),
            vmem((N, CH), BF16),
            vmem((4, 4, 32, N), F32),
            vmem((8, 2, 32, N), F32),
            vmem((4, 32, N), F32),
            vmem((4, 3, N, N), F32),
            vmem((4, 4, 3, 8, N), F32),
            vmem((4, 4, 8, N), F32),
            vmem((8, 2, 8, N), F32),
            vmem((RADIAL * N, HALO), F32),
            pltpu.SemaphoreType.DMA((4, 8)),
            pltpu.SemaphoreType.DMA((4, 8)),
        ],
        compiler_params=pltpu.CompilerParams(
            collective_id=0, has_side_effects=True, vmem_limit_bytes=56 * 1024 * 1024
        ),
    )(positions, valid_mask, species, density_table, radial_gain, readout)
    return forces[:, :, :3].transpose(2, 0, 1, 3), energies.transpose(2, 0, 1, 3)


def solution(mesh):
    nx, ny = mesh.shape["gx"], mesh.shape["gy"]
    in_specs = (P(None, "gx", "gy", None), P("gx", "gy", None), P("gx", "gy", None), P(), P(), P())
    out_specs = (P(None, "gx", "gy", None), P(None, "gx", "gy", None))
    return jax.shard_map(
        functools.partial(shards, nx, ny), mesh=mesh, in_specs=in_specs, out_specs=out_specs,
        check_vma=False,
    )
```

```python
import functools
import math

import jax
import jax.numpy as jnp
from jax import lax
from jax.experimental import pallas as pl
from jax.experimental.pallas import tpu as pltpu
from jax.sharding import PartitionSpec as P

MESH = pl.DeviceIdType.MESH
F32 = jnp.float32
BF16 = jnp.bfloat16

RADIAL = 8
SPECIES = 4
HEADS = 16
N = 128
CH = 256
CUT = 6.0
SOFT = 0.01
SPACE = CUT / (RADIAL - 1)
COEF = [math.exp(8.0 * k - k * k) for k in range(RADIAL)]
DIRS = [(dx, dy) for dx in (-1, 0, 1) for dy in (-1, 0, 1) if (dx, dy) != (0, 0)]
OWN = 4 * N
HALO = 5 * N
ROWS = 32
BLOCKS = N // ROWS


def nn(a, b):
    return lax.dot_general(a, b, (((1,), (0,)), ((), ())), preferred_element_type=F32)


def tn(a, b):
    return lax.dot_general(a, b, (((0,), (0,)), ((), ())), preferred_element_type=F32)


def nt(a, b):
    return lax.dot_general(a, b, (((1,), (1,)), ((), ())), preferred_element_type=F32)


def border(d):
    return {1: 2, -1: 1, 0: pl.ds(1, 2)}[d]


def landing(d):
    return {1: 0, -1: 3, 0: pl.ds(1, 2)}[d]


def beyond(d):
    return {1: 3, -1: 0, 0: pl.ds(1, 2)}[d]


def own_slot(c):
    return 1 + c // 2, 1 + c % 2


def halo_slots(c):
    a_out, b_out = 3 * (c // 2), 3 * (c % 2)
    return [(a_out, b_out), (a_out, 1), (a_out, 2), (1, b_out), (2, b_out)]


def loop(steps, body):
    lax.fori_loop(0, steps, body, 0)


def sigmoid(x):
    return 1.0 / (1.0 + jnp.exp(-x))


def kernel(
    nx, ny,
    pos_ref, valid_ref, spec_ref, table_ref, gain_ref, readout_ref,
    forces_ref, energies_ref,
    atoms, xi, basis_0, basis_1, basis_2, basis_3, u_s, a_s, rc_s, ri_s, dens, hid, hid_own, slope,
    msg, gms, tab_t, tab_s, gk, read_t, second, back_t, gm_own, gm_b,
    gpart, grecv, gsum, fi, fj, fpart, frecv, gs_a, gs_b,
    send_sem, recv_sem,
):
    gx, gy = lax.axis_index("gx"), lax.axis_index("gy")
    basis = (basis_0, basis_1, basis_2, basis_3)
    own_slots = [own_slot(c) for c in range(4)]

    def there(dx, dy):
        ok = None
        for d, g, n in ((dx, gx, nx), (dy, gy, ny)):
            if d:
                one = (g < n - 1) if d > 0 else (g > 0)
                ok = one if ok is None else jnp.logical_and(ok, one)
        return ok

    def copy(r, n, src, dst, peer):
        return pltpu.make_async_remote_copy(
            src_ref=src, dst_ref=dst, send_sem=send_sem.at[r, n], recv_sem=recv_sem.at[r, n],
            device_id=peer, device_id_type=MESH,
        )

    def outward(r, buf, wait):
        for n, (dx, dy) in enumerate(DIRS):
            src = buf.at[border(dx), border(dy)]
            dst = buf.at[landing(dx), landing(dy)]
            if wait == "recv":
                @pl.when(there(-dx, -dy))
                def _():
                    copy(r, n, src, dst, (gx - dx, gy - dy)).wait_recv()
            else:
                @pl.when(there(dx, dy))
                def _():
                    c = copy(r, n, src, dst, (gx + dx, gy + dy))
                    c.start() if wait == "start" else c.wait_send()

    def inward(r, buf, land, wait):
        for n, (dx, dy) in enumerate(DIRS):
            src = buf.at[beyond(dx), beyond(dy)]
            dst = land.at[n, 0] if dx and dy else land.at[n]
            if wait == "recv":
                @pl.when(there(-dx, -dy))
                def _():
                    copy(r, n, src, dst, (gx - dx, gy - dy)).wait_recv()
            else:
                @pl.when(there(dx, dy))
                def _():
                    c = copy(r, n, src, dst, (gx + dx, gy + dy))
                    c.start() if wait == "start" else c.wait_send()

    def returned(land, a, b):
        total = None
        for n, (dx, dy) in enumerate(DIRS):
            if (dx == 0 or a == (1 if dx == 1 else 2)) and (dy == 0 or b == (1 if dy == 1 else 2)):
                m = a - 1 if dx == 0 else (b - 1 if dy == 0 else 0)
                total = land[n, m] if total is None else total + land[n, m]
        return total

    for a in range(4):
        for b in range(4):
            if a in (1, 2) and b in (1, 2):
                rows = [pos_ref[i, a - 1, b - 1 : b, :] for i in range(3)]
                rows.append(valid_ref[a - 1, b - 1 : b, :].astype(F32))
                rows.append(spec_ref[a - 1, b - 1 : b, :].astype(F32))
                rows.append(jnp.zeros((3, N), F32))
                atoms[a, b] = jnp.concatenate(rows, 0)
            else:
                atoms[a, b] = jnp.zeros((8, N), F32)
                dens[a, b] = jnp.zeros((RADIAL * SPECIES, N), F32)
    grecv[...] = jnp.zeros_like(grecv)
    frecv[...] = jnp.zeros_like(frecv)

    barrier = pltpu.get_barrier_semaphore()
    for dx, dy in DIRS:
        @pl.when(there(dx, dy))
        def _():
            pl.semaphore_signal(barrier, inc=1, device_id=(gx + dx, gy + dy), device_id_type=MESH)
    span_x = 1 + jnp.where(gx > 0, 1, 0) + jnp.where(gx < nx - 1, 1, 0)
    span_y = 1 + jnp.where(gy > 0, 1, 0) + jnp.where(gy < ny - 1, 1, 0)

    table = table_ref[...] * 0.125
    high = table.astype(BF16).astype(F32)
    low = table - high
    tab_s[...] = jnp.concatenate([high, low], 0).astype(BF16)
    stacked = jnp.concatenate([high, high, low, jnp.zeros((32, CH), F32)], 0)
    tab_t[...] = stacked.astype(BF16)
    for k in range(RADIAL):
        row = gain_ref[k : k + 1, :] * (COEF[k] / 32.0)
        gk[k] = row
    read_t[...] = jnp.concatenate([readout_ref[...], jnp.zeros((N - HEADS, CH), BF16)], 0)
    for c in range(4):
        a, b = own_slot(c)
        tile = atoms[a, b]
        x = jnp.where(tile[3:4] > 0.0, tile[0:1], 1e4)
        xi[c, 0] = jnp.broadcast_to(x, (N, N)).T
        xi[c, 1] = jnp.broadcast_to(tile[1:2], (N, N)).T
        xi[c, 2] = jnp.broadcast_to(tile[2:3], (N, N)).T

    pl.semaphore_wait(barrier, span_x * span_y - 1)
    outward(0, atoms, "start")

    def offsets(c, rows, a, b):
        xj = jnp.where(atoms[a, b, 3:4, :] > 0.0, atoms[a, b, 0:1, :], -1e4)
        dx = xi[c, 0, rows, :] - xj
        dy = xi[c, 1, rows, :] - atoms[a, b, 1:2, :]
        dz = xi[c, 2, rows, :] - atoms[a, b, 2:3, :]
        return dx, dy, dz

    def pair_basis(c, block, a, b, lane, self_cell):
        rows = slice(block * ROWS, (block + 1) * ROWS)
        cols = slice(lane, lane + N)
        dx, dy, dz = offsets(c, rows, a, b)
        sq = dx * dx + dy * dy + (dz * dz + SOFT)
        if self_cell:
            i = lax.broadcasted_iota(jnp.int32, (ROWS, N), 0) + block * ROWS
            j = lax.broadcasted_iota(jnp.int32, (ROWS, N), 1)
            sq = jnp.where(i == j, 1e8, sq)
        ri = lax.rsqrt(sq)
        reach = jnp.maximum(1.0 - sq * (1.0 / (CUT * CUT)), 0.0)
        t = jnp.minimum(sq * ri * (1.0 / SPACE), float(RADIAL - 1))
        u = jnp.exp(2.0 * t - 8.0)
        amp = jnp.exp(-(t * t)) * reach
        u_s[c, rows, cols] = u
        a_s[c, rows, cols] = amp
        rc_s[c, rows, cols] = reach
        ri_s[c, rows, cols] = ri
        term = amp * reach
        for k in range(RADIAL):
            basis[c][k * N + block * ROWS : k * N + (block + 1) * ROWS, cols] = term.astype(BF16)
            if k < RADIAL - 1:
                term = term * u

    def own_pairs(c):
        for block in range(BLOCKS):
            for j, (a, b) in enumerate(own_slots):
                pair_basis(c, block, a, b, j * N, c == j)

    def halo_pairs(c):
        for block in range(BLOCKS):
            for m, (a, b) in enumerate(halo_slots(c)):
                pair_basis(c, block, a, b, OWN + m * N, False)

    def kinds(a, b, rows):
        kind = atoms[a, b, 4:5, :].astype(jnp.int32)
        r = lax.broadcasted_iota(jnp.int32, (rows, N), 0)
        return r, kind

    def selector(a, b):
        r, kind = kinds(a, b, N)
        hit = jnp.logical_and(r < 64, (r & 3) == kind)
        hid[a, b, :, CH:] = jnp.where(hit, 1.0, 0.0).T.astype(BF16)

    def hot(slots):
        parts = []
        for a, b in slots:
            r, kind = kinds(a, b, 16)
            parts.append(jnp.where(r == kind, 1.0, 0.0).astype(BF16))
        return jnp.concatenate(parts, 1)

    def own_density(c):
        out = nt(hot(own_slots), basis[c][:, 0:OWN])
        a, b = own_slots[c]
        for k in range(RADIAL):
            dens[a, b, k * SPECIES : (k + 1) * SPECIES, :] = (
                out[0:SPECIES, k * N : (k + 1) * N] * COEF[k]
            )

    def halo_density(c):
        out = nt(hot(halo_slots(c)), basis[c][:, OWN:])
        a, b = own_slots[c]
        for k in range(RADIAL):
            dens[a, b, k * SPECIES : (k + 1) * SPECIES, :] += (
                out[0:SPECIES, k * N : (k + 1) * N] * COEF[k]
            )

    own_pairs(0)
    for c in range(1, 4):
        own_pairs(c)
        own_density(c - 1)
    for a, b in own_slots:
        selector(a, b)
    outward(0, atoms, "recv")
    for c in range(4):
        for m in range(3):
            selector(*[(0, m), (3, m + 1), (m + 1, 0), (m, 3)][c])
        halo_pairs(c)
        halo_density(c - 1) if c else own_density(3)
    halo_density(3)
    outward(1, dens, "start")

    def features(slots):
        parts = []
        for a, b in slots:
            d = dens[a, b]
            top = d.astype(BF16)
            rest = (d - top.astype(F32)).astype(BF16)
            parts.append(jnp.concatenate([top, rest, top, jnp.zeros((32, N), BF16)], 0))
        z = tn(jnp.concatenate(parts, 1), tab_t[...])
        s = sigmoid(z)
        h = z * s
        sp = s * (1.0 + z * (1.0 - s))
        for m, (a, b) in enumerate(slots):
            rows = slice(m * N, (m + 1) * N)
            hid[a, b, :, 0:CH] = h[rows].astype(BF16)
            slope[a, b] = sp[rows]
        return h

    h = features(own_slots)
    for c in range(4):
        hid_own[c] = h[c * N : (c + 1) * N]

    def gained(prod):
        total = prod[0:N] * gk[0]
        for k in range(1, RADIAL):
            total = total + prod[k * N : (k + 1) * N] * gk[k]
        return total

    h = jnp.concatenate([hid[a, b, :, 0:CH] for a, b in own_slots], 0)
    for c in range(4):
        msg[c] = gained(nn(basis[c][:, 0:OWN], h))
    outward(1, dens, "recv")

    features([(0, b) for b in range(4)])
    features([(3, b) for b in range(4)])
    features([(1, 0), (2, 0), (1, 3), (2, 3)])

    for c in range(4):
        h = jnp.concatenate([hid[a, b, :, 0:CH] for a, b in halo_slots(c)], 0)
        p = msg[c] + gained(nn(basis[c][:, OWN:], h)) + hid_own[c]
        s = sigmoid(p)
        second[c * N : (c + 1) * N, :] = (p * s).astype(BF16)
        msg[c] = s * (1.0 + p * (1.0 - s))

    heads = nt(read_t[0:HEADS, :], second[...])
    sh = sigmoid(heads)
    valid = jnp.concatenate([atoms[a, b, 3:4, :] for a, b in own_slots], 1)
    out = valid * (heads * sh)
    back = (valid * (1.0 / HEADS)) * (sh * (1.0 + heads * (1.0 - sh)))
    for c, (a, b) in enumerate(own_slots):
        cols = slice(c * N, (c + 1) * N)
        for h in range(HEADS):
            energies_ref[h, a - 1, b - 1 : b, :] = out[h : h + 1, cols]
        tile = jnp.concatenate([back[:, cols], jnp.zeros((N - HEADS, N), F32)], 0)
        back_t[c] = tile.T.astype(BF16)

    def project(x):
        out = nt(tab_s[...], x)
        return out[0:32] + out[32:64]

    def head_grad(c):
        dsec = nn(back_t[c], read_t[...]).astype(BF16).astype(F32)
        gm = dsec * msg[c]
        gm_own[c] = gm
        gm_b[c * N : (c + 1) * N, :] = gm.astype(BF16)
        for k in range(RADIAL):
            gms[c, k * N : (k + 1) * N, 0:CH] = (gm * gk[k]).astype(BF16)

    def halo_grad(c):
        x = tn(basis[c][:, OWN:], gms[c, :, 0:CH])
        slots = halo_slots(c)
        x = x * jnp.concatenate([slope[a, b] for a, b in slots], 0)
        out = project(x.astype(BF16))
        for m, (a, b) in enumerate(slots):
            gpart[a, b] += out[:, m * N : (m + 1) * N]

    gpart[...] = jnp.zeros_like(gpart)
    head_grad(0)
    for c in range(4):
        if c < 3:
            head_grad(c + 1)
        halo_grad(c)
    inward(2, gpart, grecv, "start")

    for c, (a, b) in enumerate(own_slots):
        x = gained(nn(basis[c][:, 0:OWN], gm_b[...])) + gm_own[c]
        gsum[c] = project((x * slope[a, b]).astype(BF16))
    inward(2, gpart, grecv, "recv")

    for c in range(4):
        a, b = own_slot(c)
        g = gsum[c] + returned(grecv, a, b)
        r = lax.broadcasted_iota(jnp.int32, (32, N), 0) >> 2
        coef = jnp.full((32, N), COEF[0], F32)
        for k in range(1, RADIAL):
            coef = jnp.where(r == k, COEF[k], coef)
        g = g * coef
        top = g.astype(BF16).astype(F32)
        gt = jnp.concatenate([top, g - top, jnp.zeros((64, N), F32)], 0).T
        lane = lax.broadcasted_iota(jnp.int32, (N, N), 1)
        for k in range(RADIAL):
            keep = jnp.logical_and(lane < 64, ((lane & 31) >> 2) == k)
            gms[c, k * N : (k + 1) * N, CH:] = jnp.where(keep, gt, 0.0).astype(BF16)

    fj[...] = jnp.zeros_like(fj)

    def gradients(step, buf):
        c = step % 4
        slots = halo_slots(c) if step < 4 else own_slots
        h = jnp.concatenate([hid[a, b] for a, b in slots], 0)
        buf[:, 0 : h.shape[0]] = nt(gms[c], h)

    def block_forces(c, block, slots, lane0, buf):
        rows = slice(block * ROWS, (block + 1) * ROWS)
        sums = [jnp.zeros((ROWS, N), F32) for _ in range(3)]
        for m, (a, b) in enumerate(slots):
            cols = slice(lane0 + m * N, lane0 + (m + 1) * N)
            u = u_s[c, rows, cols]

            def grad(k):
                return buf[k * N + block * ROWS : k * N + (block + 1) * ROWS, m * N : (m + 1) * N]

            poly = grad(RADIAL - 1)
            slant = poly
            for k in range(RADIAL - 2, -1, -1):
                poly = poly * u + grad(k)
                if k:
                    slant = slant * u + poly
            slant = slant * u
            reach = rc_s[c, rows, cols]
            inner = ri_s[c, rows, cols] * slant * (2.0 / SPACE) - poly * (2.0 / SPACE**2)
            force = a_s[c, rows, cols] * (reach * inner - poly * (4.0 / CUT**2))
            for i, d in enumerate(offsets(c, rows, a, b)):
                f = force * d
                sums[i] = sums[i] + f
                part = f[0:8]
                for q in range(1, ROWS // 8):
                    part = part + f[8 * q : 8 * q + 8]
                fj[a, b, i] += part
        for i in range(3):
            if lane0:
                fi[c, i, rows, :] = sums[i]
            else:
                fi[c, i, rows, :] += sums[i]

    def pair_forces(step, buf):
        c = step % 4
        slots, lane0 = (halo_slots(c), OWN) if step < 4 else (own_slots, 0)
        for block in range(BLOCKS):
            block_forces(c, block, slots, lane0, buf)

    bufs = (gs_a, gs_b)
    gradients(0, gs_a)
    for step in range(4):
        pair_forces(step, bufs[step % 2])
        gradients(step + 1, bufs[(step + 1) % 2])
    for a in range(4):
        for b in range(4):
            if not (a in (1, 2) and b in (1, 2)):
                rows = [jnp.sum(fj[a, b, i], 0, keepdims=True) for i in range(3)]
                fpart[a, b] = jnp.concatenate(rows + [jnp.zeros((5, N), F32)], 0)
    inward(3, fpart, frecv, "start")
    for step in range(4, 8):
        pair_forces(step, bufs[step % 2])
        if step < 7:
            gradients(step + 1, bufs[(step + 1) % 2])
    sums = []
    for c in range(4):
        a, b = own_slot(c)
        rows = []
        for i in range(3):
            mine = jnp.sum(fi[c, i].T, 0, keepdims=True)
            rows.append(jnp.sum(fj[a, b, i], 0, keepdims=True) - mine)
        sums.append(jnp.concatenate(rows + [jnp.zeros((5, N), F32)], 0))
    inward(3, fpart, frecv, "recv")
    for c in range(4):
        a, b = own_slot(c)
        total = sums[c] + returned(frecv, a, b)
        for i in range(3):
            forces_ref[i, a - 1, b - 1 : b, :] = total[i : i + 1]
    outward(0, atoms, "send")
    outward(1, dens, "send")
    inward(2, gpart, grecv, "send")
    inward(3, fpart, frecv, "send")


def shards(nx, ny, positions, valid_mask, species, density_table, radial_gain, readout):
    vmem = pltpu.VMEM
    whole = pl.BlockSpec(memory_space=pltpu.VMEM)
    wide = OWN + HALO
    forces, energies = pl.pallas_call(
        functools.partial(kernel, nx, ny),
        out_shape=(
            jax.ShapeDtypeStruct((3, 2, 2, N), F32),
            jax.ShapeDtypeStruct((HEADS, 2, 2, N), F32),
        ),
        in_specs=[whole] * 6,
        out_specs=(whole, whole),
        scratch_shapes=[
            vmem((4, 4, 8, N), F32),
            vmem((4, 3, N, N), F32),
            vmem((RADIAL * N, wide), BF16),
            vmem((RADIAL * N, wide), BF16),
            vmem((RADIAL * N, wide), BF16),
            vmem((RADIAL * N, wide), BF16),
            vmem((4, N, wide), F32),
            vmem((4, N, wide), F32),
            vmem((4, N, wide), F32),
            vmem((4, N, wide), F32),
            vmem((4, 4, RADIAL * SPECIES, N), F32),
            vmem((4, 4, N, CH + N), BF16),
            vmem((4, N, CH), F32),
            vmem((4, 4, N, CH), F32),
            vmem((4, N, CH), F32),
            vmem((4, RADIAL * N, CH + N), BF16),
            vmem((N, CH), BF16),
            vmem((64, CH), BF16),
            vmem((RADIAL, 1, CH), F32),
            vmem((N, CH), BF16),
            vmem((OWN, CH), BF16),
            vmem((4, N, N), BF16),
            vmem((4, N, CH), F32),
            vmem((OWN, CH), BF16),
            vmem((4, 4, 32, N), F32),
            vmem((8, 2, 32, N), F32),
            vmem((4, 32, N), F32),
            vmem((4, 3, N, N), F32),
            vmem((4, 4, 3, 8, N), F32),
            vmem((4, 4, 8, N), F32),
            vmem((8, 2, 8, N), F32),
            vmem((RADIAL * N, HALO), F32),
            vmem((RADIAL * N, HALO), F32),
            pltpu.SemaphoreType.DMA((4, 8)),
            pltpu.SemaphoreType.DMA((4, 8)),
        ],
        compiler_params=pltpu.CompilerParams(
            collective_id=0, has_side_effects=True, vmem_limit_bytes=56 * 1024 * 1024
        ),
    )(positions, valid_mask, species, density_table, radial_gain, readout.T)
    return forces, energies


def solution(mesh):
    nx, ny = mesh.shape["gx"], mesh.shape["gy"]
    in_specs = (P(None, "gx", "gy", None), P("gx", "gy", None), P("gx", "gy", None), P(), P(), P())
    out_specs = (P(None, "gx", "gy", None), P(None, "gx", "gy", None))
    return jax.shard_map(
        functools.partial(shards, nx, ny), mesh=mesh, in_specs=in_specs, out_specs=out_specs,
        check_vma=False,
    )
```

```python
import functools
import math

import jax
import jax.numpy as jnp
from jax import lax
from jax.experimental import pallas as pl
from jax.experimental.pallas import tpu as pltpu
from jax.sharding import PartitionSpec as P

MESH = pl.DeviceIdType.MESH
F32 = jnp.float32
BF16 = jnp.bfloat16

RADIAL = 8
SPECIES = 4
HEADS = 16
N = 128
CH = 256
CUT = 6.0
SOFT = 0.01
SPACE = CUT / (RADIAL - 1)
COEF = [math.exp(8.0 * k - k * k) for k in range(RADIAL)]
DIRS = [(-1, -1), (-1, 1), (1, -1), (1, 1), (-1, 0), (1, 0), (0, -1), (0, 1)]
CORNERS, XSIDES, YSIDES = (0, 1, 2, 3), (4, 5), (6, 7)
OWN = 4 * N
HALO = 5 * N
ROWS = 32
BLOCKS = N // ROWS


def nn(a, b):
    return lax.dot_general(a, b, (((1,), (0,)), ((), ())), preferred_element_type=F32)


def tn(a, b):
    return lax.dot_general(a, b, (((0,), (0,)), ((), ())), preferred_element_type=F32)


def nt(a, b):
    return lax.dot_general(a, b, (((1,), (1,)), ((), ())), preferred_element_type=F32)


def border(d):
    return {1: 2, -1: 1, 0: pl.ds(1, 2)}[d]


def landing(d):
    return {1: 0, -1: 3, 0: pl.ds(1, 2)}[d]


def beyond(d):
    return {1: 3, -1: 0, 0: pl.ds(1, 2)}[d]


def own_slot(c):
    return 1 + c // 2, 1 + c % 2


def y_slots(c):
    return [(1, 3 * (c % 2)), (2, 3 * (c % 2))]


def x_slots(c):
    return [(3 * (c // 2), 1), (3 * (c // 2), 2)]


def corner_slots(c):
    return [(3 * (c // 2), 3 * (c % 2))]


def halo_slots(c):
    return y_slots(c) + x_slots(c) + corner_slots(c)


COMPLETE = ((0,), (1, 4), (2, 6), (3, 5, 7))
NEEDED = ((3, 5, 7), (2, 6), (1, 4), (0,))


PARTS = (
    (lambda c: [own_slot(j) for j in range(4)], 0, ()),
    (y_slots, OWN, YSIDES),
    (x_slots, OWN + 2 * N, XSIDES),
    (corner_slots, OWN + 4 * N, CORNERS),
)


def sigmoid(x):
    return 1.0 / (1.0 + jnp.exp(-x))


def kernel(
    nx, ny,
    pos_hbm, valid_hbm, spec_hbm, table_hbm, gain_hbm, readout_hbm,
    forces_ref, energies_ref,
    atoms, xi, basis_0, basis_1, basis_2, basis_3, u_s, a_s, rc_s, ri_s, dens, hid, hid_own, slope,
    msg, gms, tab_t, tab_s, gk, read_t, second, back_t, gm_own, gm_b,
    gpart, grecv, gsum, fi, fj, fpart, frecv, gs_a, gs_b,
    pos_ref, valid_ref, spec_ref, table_ref, gain_ref, readout_ref, load_sem,
    send_sem, recv_sem,
):
    gx, gy = lax.axis_index("gx"), lax.axis_index("gy")
    basis = (basis_0, basis_1, basis_2, basis_3)
    loads = [
        pltpu.make_async_copy(src, dst, load_sem.at[i])
        for i, (src, dst) in enumerate((
            (pos_hbm, pos_ref), (valid_hbm, valid_ref), (spec_hbm, spec_ref),
            (table_hbm, table_ref), (gain_hbm, gain_ref), (readout_hbm, readout_ref),
        ))
    ]
    for load in loads:
        load.start()
    own_slots = [own_slot(c) for c in range(4)]

    def there(dx, dy):
        ok = None
        for d, g, n in ((dx, gx, nx), (dy, gy, ny)):
            if d:
                one = (g < n - 1) if d > 0 else (g > 0)
                ok = one if ok is None else jnp.logical_and(ok, one)
        return ok

    def copy(r, n, src, dst, peer):
        return pltpu.make_async_remote_copy(
            src_ref=src, dst_ref=dst, send_sem=send_sem.at[r, n], recv_sem=recv_sem.at[r, n],
            device_id=peer, device_id_type=MESH,
        )

    def outward(r, buf, wait, dirs=range(8)):
        for n in dirs:
            dx, dy = DIRS[n]
            src = buf.at[border(dx), border(dy)]
            dst = buf.at[landing(dx), landing(dy)]
            if wait == "recv":
                @pl.when(there(-dx, -dy))
                def _():
                    copy(r, n, src, dst, (gx - dx, gy - dy)).wait_recv()
            else:
                @pl.when(there(dx, dy))
                def _():
                    c = copy(r, n, src, dst, (gx + dx, gy + dy))
                    c.start() if wait == "start" else c.wait_send()

    def inward(r, buf, land, wait, dirs=range(8)):
        for n in dirs:
            dx, dy = DIRS[n]
            src = buf.at[beyond(dx), beyond(dy)]
            dst = land.at[n, 0] if dx and dy else land.at[n]
            if wait == "recv":
                @pl.when(there(-dx, -dy))
                def _():
                    copy(r, n, src, dst, (gx - dx, gy - dy)).wait_recv()
            else:
                @pl.when(there(dx, dy))
                def _():
                    c = copy(r, n, src, dst, (gx + dx, gy + dy))
                    c.start() if wait == "start" else c.wait_send()

    def returned(land, a, b):
        total = None
        for n, (dx, dy) in enumerate(DIRS):
            if (dx == 0 or a == (1 if dx == 1 else 2)) and (dy == 0 or b == (1 if dy == 1 else 2)):
                m = a - 1 if dx == 0 else (b - 1 if dy == 0 else 0)
                total = land[n, m] if total is None else total + land[n, m]
        return total

    for a in range(4):
        for b in range(4):
            if not (a in (1, 2) and b in (1, 2)):
                atoms[a, b] = jnp.zeros((8, N), F32)
                dens[a, b] = jnp.zeros((RADIAL * SPECIES, N), F32)
    grecv[...] = jnp.zeros_like(grecv)
    frecv[...] = jnp.zeros_like(frecv)

    barrier = pltpu.get_barrier_semaphore()
    for dx, dy in DIRS:
        @pl.when(there(dx, dy))
        def _():
            pl.semaphore_signal(barrier, inc=1, device_id=(gx + dx, gy + dy), device_id_type=MESH)
    span_x = 1 + jnp.where(gx > 0, 1, 0) + jnp.where(gx < nx - 1, 1, 0)
    span_y = 1 + jnp.where(gy > 0, 1, 0) + jnp.where(gy < ny - 1, 1, 0)

    for load in loads:
        load.wait()
    for a, b in own_slots:
        rows = [pos_ref[i, a - 1, b - 1 : b, :] for i in range(3)]
        rows.append(valid_ref[a - 1, b - 1 : b, :].astype(F32))
        rows.append(spec_ref[a - 1, b - 1 : b, :].astype(F32))
        rows.append(jnp.zeros((3, N), F32))
        atoms[a, b] = jnp.concatenate(rows, 0)

    table = table_ref[...] * 0.125
    high = table.astype(BF16).astype(F32)
    low = table - high
    tab_s[...] = jnp.concatenate([high, low], 0).astype(BF16)
    stacked = jnp.concatenate([high, high, low, jnp.zeros((32, CH), F32)], 0)
    tab_t[...] = stacked.astype(BF16)
    for k in range(RADIAL):
        row = gain_ref[k : k + 1, :] * (COEF[k] / 32.0)
        gk[k] = row
    read_t[...] = jnp.concatenate([readout_ref[...], jnp.zeros((N - HEADS, CH), BF16)], 0)
    for c in range(4):
        a, b = own_slot(c)
        tile = atoms[a, b]
        x = jnp.where(tile[3:4] > 0.0, tile[0:1], 1e4)
        xi[c, 0] = jnp.broadcast_to(x, (N, N)).T
        xi[c, 1] = jnp.broadcast_to(tile[1:2], (N, N)).T
        xi[c, 2] = jnp.broadcast_to(tile[2:3], (N, N)).T

    pl.semaphore_wait(barrier, span_x * span_y - 1)
    outward(0, atoms, "start")

    def offsets(c, rows, a, b):
        xj = jnp.where(atoms[a, b, 3:4, :] > 0.0, atoms[a, b, 0:1, :], -1e4)
        dx = xi[c, 0, rows, :] - xj
        dy = xi[c, 1, rows, :] - atoms[a, b, 1:2, :]
        dz = xi[c, 2, rows, :] - atoms[a, b, 2:3, :]
        return dx, dy, dz

    def pair_basis(c, block, a, b, lane, self_cell):
        rows = slice(block * ROWS, (block + 1) * ROWS)
        cols = slice(lane, lane + N)
        dx, dy, dz = offsets(c, rows, a, b)
        sq = dx * dx + dy * dy + (dz * dz + SOFT)
        if self_cell:
            i = lax.broadcasted_iota(jnp.int32, (ROWS, N), 0) + block * ROWS
            j = lax.broadcasted_iota(jnp.int32, (ROWS, N), 1)
            sq = jnp.where(i == j, 1e8, sq)
        ri = lax.rsqrt(sq)
        reach = jnp.maximum(1.0 - sq * (1.0 / (CUT * CUT)), 0.0)
        t = jnp.minimum(sq * ri * (1.0 / SPACE), float(RADIAL - 1))
        u = jnp.exp(2.0 * t - 8.0)
        amp = jnp.exp(-(t * t)) * reach
        u_s[c, rows, cols] = u
        a_s[c, rows, cols] = amp
        rc_s[c, rows, cols] = reach
        ri_s[c, rows, cols] = ri
        term = amp * reach
        for k in range(RADIAL):
            basis[c][k * N + block * ROWS : k * N + (block + 1) * ROWS, cols] = term.astype(BF16)
            if k < RADIAL - 1:
                term = term * u

    def part_pairs(c, part):
        slots_of, lane0, _ = PARTS[part]
        for block in range(BLOCKS):
            for m, (a, b) in enumerate(slots_of(c)):
                pair_basis(c, block, a, b, lane0 + m * N, part == 0 and m == c)

    def kinds(a, b, rows):
        kind = atoms[a, b, 4:5, :].astype(jnp.int32)
        r = lax.broadcasted_iota(jnp.int32, (rows, N), 0)
        return r, kind

    def selector(a, b):
        r, kind = kinds(a, b, N)
        hit = jnp.logical_and(r < 64, (r & 3) == kind)
        hid[a, b, :, CH:] = jnp.where(hit, 1.0, 0.0).T.astype(BF16)

    def hot(slots):
        parts = []
        for a, b in slots:
            r, kind = kinds(a, b, 16)
            parts.append(jnp.where(r == kind, 1.0, 0.0).astype(BF16))
        return jnp.concatenate(parts, 1)

    def part_density(c, part):
        slots_of, lane0, _ = PARTS[part]
        slots = slots_of(c)
        out = nt(hot(slots), basis[c][:, lane0 : lane0 + len(slots) * N])
        a, b = own_slots[c]
        for k in range(RADIAL):
            rows = slice(k * SPECIES, (k + 1) * SPECIES)
            piece = out[0:SPECIES, k * N : (k + 1) * N] * COEF[k]
            dens[a, b, rows, :] = dens[a, b, rows, :] + piece if part else piece

    last = None
    for part in range(4):
        if part:
            outward(0, atoms, "recv", PARTS[part][2])
        slots_of = PARTS[part][0]
        for a, b in sorted({slot for c in range(4) for slot in slots_of(c)}):
            selector(a, b)
        for c in range(4):
            part_pairs(c, part)
            if last:
                part_density(*last)
            last = (c, part)
    part_density(*last)
    outward(1, dens, "start")

    def features(slots):
        parts = []
        for a, b in slots:
            d = dens[a, b]
            top = d.astype(BF16)
            rest = (d - top.astype(F32)).astype(BF16)
            parts.append(jnp.concatenate([top, rest, top, jnp.zeros((32, N), BF16)], 0))
        z = tn(jnp.concatenate(parts, 1), tab_t[...])
        s = sigmoid(z)
        h = z * s
        sp = s * (1.0 + z * (1.0 - s))
        for m, (a, b) in enumerate(slots):
            rows = slice(m * N, (m + 1) * N)
            hid[a, b, :, 0:CH] = h[rows].astype(BF16)
            slope[a, b] = sp[rows]
        return h

    h = features(own_slots)
    for c in range(4):
        hid_own[c] = h[c * N : (c + 1) * N]

    def gained(prod):
        total = prod[0:N] * gk[0]
        for k in range(1, RADIAL):
            total = total + prod[k * N : (k + 1) * N] * gk[k]
        return total

    def part_message(c, part):
        slots_of, lane0, _ = PARTS[part]
        slots = slots_of(c)
        h = jnp.concatenate([hid[a, b, :, 0:CH] for a, b in slots], 0)
        return gained(nn(basis[c][:, lane0 : lane0 + len(slots) * N], h))

    for c in range(4):
        msg[c] = part_message(c, 0) + hid_own[c]
    for part in (1, 2):
        outward(1, dens, "recv", PARTS[part][2])
        features(sorted({slot for c in range(4) for slot in PARTS[part][0](c)}))
        for c in range(4):
            msg[c] += part_message(c, part)
    outward(1, dens, "recv", CORNERS)
    features([corner_slots(c)[0] for c in range(4)])
    for c in range(4):
        p = msg[c] + part_message(c, 3)
        s = sigmoid(p)
        second[c * N : (c + 1) * N, :] = (p * s).astype(BF16)
        msg[c] = s * (1.0 + p * (1.0 - s))

    heads = nt(read_t[0:HEADS, :], second[...])
    sh = sigmoid(heads)
    valid = jnp.concatenate([atoms[a, b, 3:4, :] for a, b in own_slots], 1)
    out = valid * (heads * sh)
    back = (valid * (1.0 / HEADS)) * (sh * (1.0 + heads * (1.0 - sh)))
    for c, (a, b) in enumerate(own_slots):
        cols = slice(c * N, (c + 1) * N)
        for h in range(HEADS):
            energies_ref[h, a - 1, b - 1 : b, :] = out[h : h + 1, cols]
        tile = jnp.concatenate([back[:, cols], jnp.zeros((N - HEADS, N), F32)], 0)
        back_t[c] = tile.T.astype(BF16)

    def project(x):
        out = nt(tab_s[...], x)
        return out[0:32] + out[32:64]

    def head_grad(c):
        dsec = nn(back_t[c], read_t[...]).astype(BF16).astype(F32)
        gm = dsec * msg[c]
        gm_own[c] = gm
        gm_b[c * N : (c + 1) * N, :] = gm.astype(BF16)
        for k in range(RADIAL):
            gms[c, k * N : (k + 1) * N, 0:CH] = (gm * gk[k]).astype(BF16)

    def halo_grad(c):
        x = tn(basis[c][:, OWN:], gms[c, :, 0:CH])
        slots = halo_slots(c)
        x = x * jnp.concatenate([slope[a, b] for a, b in slots], 0)
        out = project(x.astype(BF16))
        for m, (a, b) in enumerate(slots):
            gpart[a, b] += out[:, m * N : (m + 1) * N]

    gpart[...] = jnp.zeros_like(gpart)
    head_grad(0)
    for c in range(4):
        if c < 3:
            head_grad(c + 1)
        halo_grad(c)
        inward(2, gpart, grecv, "start", COMPLETE[c])

    for c, (a, b) in enumerate(own_slots):
        x = gained(nn(basis[c][:, 0:OWN], gm_b[...])) + gm_own[c]
        gsum[c] = project((x * slope[a, b]).astype(BF16))
    def density_grad(c):
        inward(2, gpart, grecv, "recv", NEEDED[c])
        a, b = own_slot(c)
        g = gsum[c] + returned(grecv, a, b)
        r = lax.broadcasted_iota(jnp.int32, (32, N), 0) >> 2
        coef = jnp.full((32, N), COEF[0], F32)
        for k in range(1, RADIAL):
            coef = jnp.where(r == k, COEF[k], coef)
        g = g * coef
        top = g.astype(BF16).astype(F32)
        gt = jnp.concatenate([top, g - top, jnp.zeros((64, N), F32)], 0).T
        lane = lax.broadcasted_iota(jnp.int32, (N, N), 1)
        for k in range(RADIAL):
            keep = jnp.logical_and(lane < 64, ((lane & 31) >> 2) == k)
            gms[c, k * N : (k + 1) * N, CH:] = jnp.where(keep, gt, 0.0).astype(BF16)

    fj[...] = jnp.zeros_like(fj)

    def gradients(step, buf):
        c = step % 4
        slots = halo_slots(c) if step < 4 else own_slots
        h = jnp.concatenate([hid[a, b] for a, b in slots], 0)
        buf[:, 0 : h.shape[0]] = nt(gms[c], h)

    def block_forces(c, block, slots, lane0, buf):
        rows = slice(block * ROWS, (block + 1) * ROWS)
        sums = [jnp.zeros((ROWS, N), F32) for _ in range(3)]
        for m, (a, b) in enumerate(slots):
            cols = slice(lane0 + m * N, lane0 + (m + 1) * N)
            u = u_s[c, rows, cols]

            def grad(k):
                return buf[k * N + block * ROWS : k * N + (block + 1) * ROWS, m * N : (m + 1) * N]

            poly = grad(RADIAL - 1)
            slant = poly
            for k in range(RADIAL - 2, -1, -1):
                poly = poly * u + grad(k)
                if k:
                    slant = slant * u + poly
            slant = slant * u
            reach = rc_s[c, rows, cols]
            inner = ri_s[c, rows, cols] * slant * (2.0 / SPACE) - poly * (2.0 / SPACE**2)
            force = a_s[c, rows, cols] * (reach * inner - poly * (4.0 / CUT**2))
            for i, d in enumerate(offsets(c, rows, a, b)):
                f = force * d
                sums[i] = sums[i] + f
                part = f[0:8]
                for q in range(1, ROWS // 8):
                    part = part + f[8 * q : 8 * q + 8]
                fj[a, b, i] += part
        for i in range(3):
            if lane0:
                fi[c, i, rows, :] = sums[i]
            else:
                fi[c, i, rows, :] += sums[i]

    def pair_forces(step, buf):
        c = step % 4
        slots, lane0 = (halo_slots(c), OWN) if step < 4 else (own_slots, 0)
        for block in range(BLOCKS):
            block_forces(c, block, slots, lane0, buf)

    def halo_force(n):
        dx, dy = DIRS[n]
        for a in {1: (3,), -1: (0,), 0: (1, 2)}[dx]:
            for b in {1: (3,), -1: (0,), 0: (1, 2)}[dy]:
                rows = [jnp.sum(fj[a, b, i], 0, keepdims=True) for i in range(3)]
                fpart[a, b] = jnp.concatenate(rows + [jnp.zeros((5, N), F32)], 0)

    bufs = (gs_a, gs_b)
    density_grad(0)
    gradients(0, gs_a)
    for step in range(4):
        if step < 3:
            density_grad(step + 1)
        pair_forces(step, bufs[step % 2])
        gradients(step + 1, bufs[(step + 1) % 2])
        for n in COMPLETE[step]:
            halo_force(n)
        inward(3, fpart, frecv, "start", COMPLETE[step])
    for step in range(4, 8):
        pair_forces(step, bufs[step % 2])
        if step < 7:
            gradients(step + 1, bufs[(step + 1) % 2])
    sums = []
    for c in range(4):
        a, b = own_slot(c)
        rows = []
        for i in range(3):
            mine = jnp.sum(fi[c, i].T, 0, keepdims=True)
            rows.append(jnp.sum(fj[a, b, i], 0, keepdims=True) - mine)
        sums.append(jnp.concatenate(rows + [jnp.zeros((5, N), F32)], 0))
    inward(3, fpart, frecv, "recv")
    for c in range(4):
        a, b = own_slot(c)
        total = sums[c] + returned(frecv, a, b)
        for i in range(3):
            forces_ref[i, a - 1, b - 1 : b, :] = total[i : i + 1]
    outward(0, atoms, "send")
    outward(1, dens, "send")
    inward(2, gpart, grecv, "send")
    inward(3, fpart, frecv, "send")


def hand_over(forces_ref, energies_ref, forces_out, energies_out):
    forces_out[...] = forces_ref[...]
    energies_out[...] = energies_ref[...]


def shards(nx, ny, positions, valid_mask, species, density_table, radial_gain, readout):
    vmem = pltpu.VMEM
    whole = pl.BlockSpec(memory_space=pltpu.VMEM)
    wide = OWN + HALO
    forces, energies = pl.pallas_call(
        functools.partial(kernel, nx, ny),
        out_shape=(
            pltpu.VMEM((3, 2, 2, N), F32),
            pltpu.VMEM((HEADS, 2, 2, N), F32),
        ),
        in_specs=[pl.BlockSpec(memory_space=pl.ANY)] * 6,
        out_specs=(whole, whole),
        scratch_shapes=[
            vmem((4, 4, 8, N), F32),
            vmem((4, 3, N, N), F32),
            vmem((RADIAL * N, wide), BF16),
            vmem((RADIAL * N, wide), BF16),
            vmem((RADIAL * N, wide), BF16),
            vmem((RADIAL * N, wide), BF16),
            vmem((4, N, wide), F32),
            vmem((4, N, wide), F32),
            vmem((4, N, wide), F32),
            vmem((4, N, wide), F32),
            vmem((4, 4, RADIAL * SPECIES, N), F32),
            vmem((4, 4, N, CH + N), BF16),
            vmem((4, N, CH), F32),
            vmem((4, 4, N, CH), F32),
            vmem((4, N, CH), F32),
            vmem((4, RADIAL * N, CH + N), BF16),
            vmem((N, CH), BF16),
            vmem((64, CH), BF16),
            vmem((RADIAL, 1, CH), F32),
            vmem((N, CH), BF16),
            vmem((OWN, CH), BF16),
            vmem((4, N, N), BF16),
            vmem((4, N, CH), F32),
            vmem((OWN, CH), BF16),
            vmem((4, 4, 32, N), F32),
            vmem((8, 2, 32, N), F32),
            vmem((4, 32, N), F32),
            vmem((4, 3, N, N), F32),
            vmem((4, 4, 3, 8, N), F32),
            vmem((4, 4, 8, N), F32),
            vmem((8, 2, 8, N), F32),
            vmem((RADIAL * N, HALO), F32),
            vmem((RADIAL * N, HALO), F32),
            vmem((3, 2, 2, N), F32),
            vmem((2, 2, N), jnp.int32),
            vmem((2, 2, N), jnp.int32),
            vmem((RADIAL * SPECIES, CH), F32),
            vmem((RADIAL, CH), F32),
            vmem((HEADS, CH), BF16),
            pltpu.SemaphoreType.DMA((6,)),
            pltpu.SemaphoreType.DMA((4, 8)),
            pltpu.SemaphoreType.DMA((4, 8)),
        ],
        compiler_params=pltpu.CompilerParams(
            collective_id=0, has_side_effects=True, vmem_limit_bytes=56 * 1024 * 1024
        ),
    )(positions, valid_mask, species, density_table, radial_gain, readout.T)
    return forces, energies


def solution(mesh):
    nx, ny = mesh.shape["gx"], mesh.shape["gy"]
    in_specs = (P(None, "gx", "gy", None), P("gx", "gy", None), P("gx", "gy", None), P(), P(), P())
    out_specs = (P(None, "gx", "gy", None), P(None, "gx", "gy", None))
    return jax.shard_map(
        functools.partial(shards, nx, ny), mesh=mesh, in_specs=in_specs, out_specs=out_specs,
        check_vma=False,
    )
```

```python
import functools
import math

import jax
import jax.numpy as jnp
from jax import lax
from jax.experimental import pallas as pl
from jax.experimental.pallas import tpu as pltpu
from jax.sharding import PartitionSpec as P

MESH = pl.DeviceIdType.MESH
F32 = jnp.float32
BF16 = jnp.bfloat16

RADIAL = 8
SPECIES = 4
HEADS = 16
N = 128
CH = 256
CUT = 6.0
SOFT = 0.01
SPACE = CUT / (RADIAL - 1)
COEF = [math.exp(8.0 * k - k * k) for k in range(RADIAL)]
DIRS = [(-1, -1), (-1, 1), (1, -1), (1, 1), (-1, 0), (1, 0), (0, -1), (0, 1)]
OWN = 4 * N
HALO = 5 * N
ROWS = 32
BLOCKS = N // ROWS


def nn(a, b):
    return lax.dot_general(a, b, (((1,), (0,)), ((), ())), preferred_element_type=F32)


def tn(a, b):
    return lax.dot_general(a, b, (((0,), (0,)), ((), ())), preferred_element_type=F32)


def nt(a, b):
    return lax.dot_general(a, b, (((1,), (1,)), ((), ())), preferred_element_type=F32)


def border(d):
    return {1: 2, -1: 1, 0: pl.ds(1, 2)}[d]


def landing(d):
    return {1: 0, -1: 3, 0: pl.ds(1, 2)}[d]


def beyond(d):
    return {1: 3, -1: 0, 0: pl.ds(1, 2)}[d]


def own_slot(c):
    return 1 + c // 2, 1 + c % 2


def y_slots(c):
    return [(1, 3 * (c % 2)), (2, 3 * (c % 2))]


def x_slots(c):
    a = 3 * (c // 2)
    return [(a, 1), (a, 2), (a, 3 * (c % 2))]


def halo_slots(c):
    return y_slots(c) + x_slots(c)


GRAD_ORDER = ((0, (0,)), (1, (1, 4)), (2, (2, 6)), (3, (3, 5, 7)))
NEEDED = {2: (1, 4, 7), 3: (0, 6), 0: (3, 5), 1: (2,)}


PARTS = (
    (range(4), lambda c: [own_slot(j) for j in range(4)], 0, ()),
    (range(4), y_slots, OWN, (6, 7)),
    ((2, 3), x_slots, OWN + 2 * N, (4, 0, 1)),
    ((0, 1), x_slots, OWN + 2 * N, (5, 2, 3)),
)


def sigmoid(x):
    return 1.0 / (1.0 + jnp.exp(-x))


def kernel(
    nx, ny,
    pos_hbm, valid_hbm, spec_hbm, table_hbm, gain_hbm, readout_hbm,
    forces_ref, energies_ref,
    atoms, xi, basis_0, basis_1, basis_2, basis_3, u_s, a_s, rc_s, ri_s, dens, hid, hid_own, slope,
    msg, gms, tab_t, tab_s, gk, read_t, second, back_t, gm_own, gm_b,
    gpart, grecv, gsum, fi, fj, fpart, frecv, gs_a, gs_b, poly_s, slant_s,
    pos_ref, valid_ref, spec_ref, table_ref, gain_ref, readout_ref, load_sem,
    send_sem, recv_sem,
):
    gx, gy = lax.axis_index("gx"), lax.axis_index("gy")
    basis = (basis_0, basis_1, basis_2, basis_3)
    loads = [
        pltpu.make_async_copy(src, dst, load_sem.at[i])
        for i, (src, dst) in enumerate((
            (pos_hbm, pos_ref), (valid_hbm, valid_ref), (spec_hbm, spec_ref),
            (table_hbm, table_ref), (gain_hbm, gain_ref), (readout_hbm, readout_ref),
        ))
    ]
    for load in loads:
        load.start()
    own_slots = [own_slot(c) for c in range(4)]

    def turn(g):
        return jnp.where((g + 4) % 4 >= 2, -1, 1)

    side = turn(gx)
    own_row = {1: jnp.where(side > 0, 0, 1), 2: jnp.where(side > 0, 1, 0)}

    def peer(dx, dy):
        return (gx + side * dx, gy + dy)

    def there(dx, dy):
        ok = None
        for d, g, n in zip((dx, dy), peer(dx, dy), (nx, ny)):
            if d:
                one = jnp.logical_and(g >= 0, g < n)
                ok = one if ok is None else jnp.logical_and(ok, one)
        return ok

    def arrival(n):
        dx, dy = DIRS[n]
        if dx == 0:
            return landing(0), n
        up = jnp.where(side * turn(gx + side * dx) * dx > 0, 1, 0)
        return 3 - 3 * up, (2 * up + (1 if dy > 0 else 0) if dy else 4 + up)

    def copy(r, n, arrived, src, dst, device):
        return pltpu.make_async_remote_copy(
            src_ref=src, dst_ref=dst, send_sem=send_sem.at[r, n], recv_sem=recv_sem.at[r, arrived],
            device_id=device, device_id_type=MESH,
        )

    def exchange(r, wait, dirs, src_of, dst_of):
        for n in dirs:
            dx, dy = DIRS[n]
            if wait == "recv":
                @pl.when(there(-dx, -dy))
                def _():
                    dst = dst_of(dx, dy, landing(dx), n)
                    copy(r, n, n, src_of(dx, dy), dst, peer(-dx, -dy)).wait_recv()
            else:
                @pl.when(there(dx, dy))
                def _():
                    row, arrived = arrival(n)
                    dst = dst_of(dx, dy, row, arrived)
                    c = copy(r, n, arrived, src_of(dx, dy), dst, peer(dx, dy))
                    c.start() if wait == "start" else c.wait_send()

    def outward(r, buf, wait, dirs=range(8)):
        exchange(
            r, wait, dirs,
            lambda dx, dy: buf.at[border(dx), border(dy)],
            lambda dx, dy, row, n: buf.at[row, landing(dy)],
        )

    def inward(r, buf, land, wait, dirs=range(8)):
        exchange(
            r, wait, dirs,
            lambda dx, dy: buf.at[beyond(dx), beyond(dy)],
            lambda dx, dy, row, n: land.at[n, 0] if dx and dy else land.at[n],
        )

    def returned(land, a, b):
        total = None
        for n, (dx, dy) in enumerate(DIRS):
            if (dx == 0 or a == (1 if dx == 1 else 2)) and (dy == 0 or b == (1 if dy == 1 else 2)):
                m = a - 1 if dx == 0 else (b - 1 if dy == 0 else 0)
                total = land[n, m] if total is None else total + land[n, m]
        return total

    for a in range(4):
        for b in range(4):
            if not (a in (1, 2) and b in (1, 2)):
                atoms[a, b] = jnp.zeros((8, N), F32)
                dens[a, b] = jnp.zeros((RADIAL * SPECIES, N), F32)
    grecv[...] = jnp.zeros_like(grecv)
    frecv[...] = jnp.zeros_like(frecv)

    barrier = pltpu.get_barrier_semaphore()
    for dx, dy in DIRS:
        @pl.when(there(dx, dy))
        def _():
            pl.semaphore_signal(barrier, inc=1, device_id=peer(dx, dy), device_id_type=MESH)
    span_x = 1 + jnp.where(gx > 0, 1, 0) + jnp.where(gx < nx - 1, 1, 0)
    span_y = 1 + jnp.where(gy > 0, 1, 0) + jnp.where(gy < ny - 1, 1, 0)

    for load in loads:
        load.wait()
    for a, b in own_slots:
        rows = [pos_ref[i, own_row[a], b - 1 : b, :] for i in range(3)]
        rows.append(valid_ref[own_row[a], b - 1 : b, :].astype(F32))
        rows.append(spec_ref[own_row[a], b - 1 : b, :].astype(F32))
        rows.append(jnp.zeros((3, N), F32))
        atoms[a, b] = jnp.concatenate(rows, 0)

    table = table_ref[...] * 0.125
    high = table.astype(BF16).astype(F32)
    low = table - high
    tab_s[...] = jnp.concatenate([high, low], 0).astype(BF16)
    stacked = jnp.concatenate([high, high, low, jnp.zeros((32, CH), F32)], 0)
    tab_t[...] = stacked.astype(BF16)
    for k in range(RADIAL):
        row = gain_ref[k : k + 1, :] * (COEF[k] / 32.0)
        gk[k] = row
    read_t[...] = jnp.concatenate([readout_ref[...], jnp.zeros((N - HEADS, CH), BF16)], 0)
    for c in range(4):
        a, b = own_slot(c)
        tile = atoms[a, b]
        x = jnp.where(tile[3:4] > 0.0, tile[0:1], 1e4)
        xi[c, 0] = jnp.broadcast_to(x, (N, N)).T
        xi[c, 1] = jnp.broadcast_to(tile[1:2], (N, N)).T
        xi[c, 2] = jnp.broadcast_to(tile[2:3], (N, N)).T

    pl.semaphore_wait(barrier, span_x * span_y - 1)
    outward(0, atoms, "start")

    def offsets(c, rows, a, b):
        xj = jnp.where(atoms[a, b, 3:4, :] > 0.0, atoms[a, b, 0:1, :], -1e4)
        dx = xi[c, 0, rows, :] - xj
        dy = xi[c, 1, rows, :] - atoms[a, b, 1:2, :]
        dz = xi[c, 2, rows, :] - atoms[a, b, 2:3, :]
        return dx, dy, dz

    def pair_basis(c, block, a, b, lane, self_cell):
        rows = slice(block * ROWS, (block + 1) * ROWS)
        cols = slice(lane, lane + N)
        dx, dy, dz = offsets(c, rows, a, b)
        sq = dx * dx + dy * dy + (dz * dz + SOFT)
        if self_cell:
            i = lax.broadcasted_iota(jnp.int32, (ROWS, N), 0) + block * ROWS
            j = lax.broadcasted_iota(jnp.int32, (ROWS, N), 1)
            sq = jnp.where(i == j, 1e8, sq)
        ri = lax.rsqrt(sq)
        reach = jnp.maximum(1.0 - sq * (1.0 / (CUT * CUT)), 0.0)
        t = jnp.minimum(sq * ri * (1.0 / SPACE), float(RADIAL - 1))
        u = jnp.exp(2.0 * t - 8.0)
        amp = jnp.exp(-(t * t)) * reach
        u_s[c, rows, cols] = u
        a_s[c, rows, cols] = amp
        rc_s[c, rows, cols] = reach
        ri_s[c, rows, cols] = ri
        term = amp * reach
        for k in range(RADIAL):
            basis[c][k * N + block * ROWS : k * N + (block + 1) * ROWS, cols] = term.astype(BF16)
            if k < RADIAL - 1:
                term = term * u

    def part_pairs(c, part):
        _, slots_of, lane0, _ = PARTS[part]
        for block in range(BLOCKS):
            for m, (a, b) in enumerate(slots_of(c)):
                pair_basis(c, block, a, b, lane0 + m * N, part == 0 and m == c)

    def kinds(a, b, rows):
        kind = atoms[a, b, 4:5, :].astype(jnp.int32)
        r = lax.broadcasted_iota(jnp.int32, (rows, N), 0)
        return r, kind

    def selector(a, b):
        r, kind = kinds(a, b, N)
        hit = jnp.logical_and(r < 64, (r & 3) == kind)
        hid[a, b, :, CH:] = jnp.where(hit, 1.0, 0.0).T.astype(BF16)

    def hot(slots):
        parts = []
        for a, b in slots:
            r, kind = kinds(a, b, 16)
            parts.append(jnp.where(r == kind, 1.0, 0.0).astype(BF16))
        return jnp.concatenate(parts, 1)

    def part_density(c, part):
        _, slots_of, lane0, _ = PARTS[part]
        slots = slots_of(c)
        out = nt(hot(slots), basis[c][:, lane0 : lane0 + len(slots) * N])
        a, b = own_slots[c]
        for k in range(RADIAL):
            rows = slice(k * SPECIES, (k + 1) * SPECIES)
            piece = out[0:SPECIES, k * N : (k + 1) * N] * COEF[k]
            dens[a, b, rows, :] = dens[a, b, rows, :] + piece if part else piece

    last = None
    for part, (cells, slots_of, _, dirs) in enumerate(PARTS):
        outward(0, atoms, "recv", dirs)
        for c in cells:
            part_pairs(c, part)
            if last:
                part_density(*last)
            last = (c, part)
        if part == 2:
            part_density(*last)
            last = None
            outward(1, dens, "start", (5, 2, 3))
    part_density(*last)
    outward(1, dens, "start", (0, 1, 4, 6, 7))
    for a in range(4):
        for b in range(4):
            selector(a, b)

    def features(slots):
        parts = []
        for a, b in slots:
            d = dens[a, b]
            top = d.astype(BF16)
            rest = (d - top.astype(F32)).astype(BF16)
            parts.append(jnp.concatenate([top, rest, top, jnp.zeros((32, N), BF16)], 0))
        z = tn(jnp.concatenate(parts, 1), tab_t[...])
        s = sigmoid(z)
        h = z * s
        sp = s * (1.0 + z * (1.0 - s))
        for m, (a, b) in enumerate(slots):
            rows = slice(m * N, (m + 1) * N)
            hid[a, b, :, 0:CH] = h[rows].astype(BF16)
            slope[a, b] = sp[rows]
        return h

    h = features(own_slots)
    for c in range(4):
        hid_own[c] = h[c * N : (c + 1) * N]

    def gained(prod):
        total = prod[0:N] * gk[0]
        for k in range(1, RADIAL):
            total = total + prod[k * N : (k + 1) * N] * gk[k]
        return total

    def part_message(c, part):
        _, slots_of, lane0, _ = PARTS[part]
        slots = slots_of(c)
        h = jnp.concatenate([hid[a, b, :, 0:CH] for a, b in slots], 0)
        return gained(nn(basis[c][:, lane0 : lane0 + len(slots) * N], h))

    for c in range(4):
        msg[c] = part_message(c, 0) + hid_own[c]
    for part in (1, 2, 3):
        cells, slots_of, _, dirs = PARTS[part]
        outward(1, dens, "recv", dirs)
        features(sorted({slot for c in cells for slot in slots_of(c)}))
        for c in cells:
            p = msg[c] + part_message(c, part)
            if part == 1:
                msg[c] = p
                continue
            s = sigmoid(p)
            second[c * N : (c + 1) * N, :] = (p * s).astype(BF16)
            msg[c] = s * (1.0 + p * (1.0 - s))

    heads = nt(read_t[0:HEADS, :], second[...])
    sh = sigmoid(heads)
    valid = jnp.concatenate([atoms[a, b, 3:4, :] for a, b in own_slots], 1)
    out = valid * (heads * sh)
    back = (valid * (1.0 / HEADS)) * (sh * (1.0 + heads * (1.0 - sh)))
    for c, (a, b) in enumerate(own_slots):
        cols = slice(c * N, (c + 1) * N)
        for h in range(HEADS):
            energies_ref[h, own_row[a], b - 1 : b, :] = out[h : h + 1, cols]
        tile = jnp.concatenate([back[:, cols], jnp.zeros((N - HEADS, N), F32)], 0)
        back_t[c] = tile.T.astype(BF16)

    def project(x):
        out = nt(tab_s[...], x)
        return out[0:32] + out[32:64]

    def head_grad(c):
        dsec = nn(back_t[c], read_t[...]).astype(BF16).astype(F32)
        gm = dsec * msg[c]
        gm_own[c] = gm
        gm_b[c * N : (c + 1) * N, :] = gm.astype(BF16)
        for k in range(RADIAL):
            gms[c, k * N : (k + 1) * N, 0:CH] = (gm * gk[k]).astype(BF16)

    def halo_grad(c):
        x = tn(basis[c][:, OWN:], gms[c, :, 0:CH])
        slots = halo_slots(c)
        x = x * jnp.concatenate([slope[a, b] for a, b in slots], 0)
        out = project(x.astype(BF16))
        for m, (a, b) in enumerate(slots):
            gpart[a, b] += out[:, m * N : (m + 1) * N]

    gpart[...] = jnp.zeros_like(gpart)
    head_grad(0)
    for c, complete in GRAD_ORDER:
        if c < 3:
            head_grad(c + 1)
        halo_grad(c)
        inward(2, gpart, grecv, "start", complete)

    def own_grad(c):
        a, b = own_slots[c]
        x = gained(nn(basis[c][:, 0:OWN], gm_b[...])) + gm_own[c]
        gsum[c] = project((x * slope[a, b]).astype(BF16))

    upper, lower, both = slice(0, CH), slice(CH, CH + N), slice(0, CH + N)

    def gradients(c, slots, lanes, buf):
        h = jnp.concatenate([hid[a, b, :, lanes] for a, b in slots], 0)
        buf[:, 0 : h.shape[0]] = nt(gms[c, :, lanes], h)

    def horner(c, block, m, lane0, buf):
        rows = slice(block * ROWS, (block + 1) * ROWS)
        u = u_s[c, rows, lane0 + m * N : lane0 + (m + 1) * N]

        def grad(k):
            return buf[k * N + block * ROWS : k * N + (block + 1) * ROWS, m * N : (m + 1) * N]

        poly = grad(RADIAL - 1)
        slant = poly
        for k in range(RADIAL - 2, -1, -1):
            poly = poly * u + grad(k)
            if k:
                slant = slant * u + poly
        return poly, slant * u

    def second_layer_sums(c, buf):
        for block in range(BLOCKS):
            rows = slice(block * ROWS, (block + 1) * ROWS)
            for m in range(5):
                cols = slice(m * N, (m + 1) * N)
                poly_s[c, rows, cols], slant_s[c, rows, cols] = horner(c, block, m, OWN, buf)

    gradients(0, halo_slots(0), upper, gs_a)
    own_grad(0)
    second_layer_sums(0, gs_a)
    gradients(1, halo_slots(1), upper, gs_b)
    own_grad(1)
    second_layer_sums(1, gs_b)
    own_grad(2)
    own_grad(3)

    def density_grad(c):
        inward(2, gpart, grecv, "recv", NEEDED[c])
        a, b = own_slot(c)
        g = gsum[c] + returned(grecv, a, b)
        r = lax.broadcasted_iota(jnp.int32, (32, N), 0) >> 2
        coef = jnp.full((32, N), COEF[0], F32)
        for k in range(1, RADIAL):
            coef = jnp.where(r == k, COEF[k], coef)
        g = g * coef
        top = g.astype(BF16).astype(F32)
        gt = jnp.concatenate([top, g - top, jnp.zeros((64, N), F32)], 0).T
        lane = lax.broadcasted_iota(jnp.int32, (N, N), 1)
        for k in range(RADIAL):
            keep = jnp.logical_and(lane < 64, ((lane & 31) >> 2) == k)
            gms[c, k * N : (k + 1) * N, CH:] = jnp.where(keep, gt, 0.0).astype(BF16)

    fj[...] = jnp.zeros_like(fj)

    def block_forces(c, block, slots, lane0, buf):
        rows = slice(block * ROWS, (block + 1) * ROWS)
        sums = [jnp.zeros((ROWS, N), F32) for _ in range(3)]
        for m, (a, b) in enumerate(slots):
            cols = slice(lane0 + m * N, lane0 + (m + 1) * N)
            poly, slant = horner(c, block, m, lane0, buf)
            if lane0 and c < 2:
                halo = slice(m * N, (m + 1) * N)
                poly = poly + poly_s[c, rows, halo]
                slant = slant + slant_s[c, rows, halo]
            reach = rc_s[c, rows, cols]
            inner = ri_s[c, rows, cols] * slant * (2.0 / SPACE) - poly * (2.0 / SPACE**2)
            force = a_s[c, rows, cols] * (reach * inner - poly * (4.0 / CUT**2))
            for i, d in enumerate(offsets(c, rows, a, b)):
                f = force * d
                sums[i] = sums[i] + f
                part = f[0:8]
                for q in range(1, ROWS // 8):
                    part = part + f[8 * q : 8 * q + 8]
                fj[a, b, i] += part
        for i in range(3):
            if lane0:
                fi[c, i, rows, :] = sums[i]
            else:
                fi[c, i, rows, :] += sums[i]

    def halo_forces(c, buf):
        for block in range(BLOCKS):
            block_forces(c, block, halo_slots(c), OWN, buf)

    def own_forces(c, buf):
        for block in range(BLOCKS):
            block_forces(c, block, own_slots, 0, buf)

    def halo_force(n):
        dx, dy = DIRS[n]
        for a in {1: (3,), -1: (0,), 0: (1, 2)}[dx]:
            for b in {1: (3,), -1: (0,), 0: (1, 2)}[dy]:
                rows = [jnp.sum(fj[a, b, i], 0, keepdims=True) for i in range(3)]
                fpart[a, b] = jnp.concatenate(rows + [jnp.zeros((5, N), F32)], 0)

    def send_forces(dirs):
        for n in dirs:
            halo_force(n)
        inward(3, fpart, frecv, "start", dirs)

    density_grad(2)
    gradients(2, halo_slots(2), both, gs_a)
    density_grad(3)
    halo_forces(2, gs_a)
    gradients(3, halo_slots(3), both, gs_b)
    send_forces((2,))
    halo_forces(3, gs_b)
    send_forces((3, 5))
    density_grad(0)
    gradients(0, halo_slots(0), lower, gs_a)
    density_grad(1)
    halo_forces(0, gs_a)
    gradients(1, halo_slots(1), lower, gs_b)
    send_forces((0, 6))
    halo_forces(1, gs_b)
    gradients(0, own_slots, both, gs_a)
    send_forces((1, 4, 7))
    own_forces(0, gs_a)
    gradients(1, own_slots, both, gs_b)
    own_forces(1, gs_b)
    gradients(2, own_slots, both, gs_a)
    own_forces(2, gs_a)
    gradients(3, own_slots, both, gs_b)
    own_forces(3, gs_b)
    sums = []
    for c in range(4):
        a, b = own_slot(c)
        rows = []
        for i in range(3):
            mine = jnp.sum(fi[c, i].T, 0, keepdims=True)
            rows.append(jnp.sum(fj[a, b, i], 0, keepdims=True) - mine)
        sums.append(jnp.concatenate(rows + [jnp.zeros((5, N), F32)], 0))
    outward(0, atoms, "send")
    outward(1, dens, "send")
    inward(2, gpart, grecv, "send")
    inward(3, fpart, frecv, "send")
    inward(3, fpart, frecv, "recv")
    for c in range(4):
        a, b = own_slot(c)
        total = sums[c] + returned(frecv, a, b)
        for i in range(3):
            forces_ref[i, own_row[a], b - 1 : b, :] = total[i : i + 1]


def shards(nx, ny, positions, valid_mask, species, density_table, radial_gain, readout):
    vmem = pltpu.VMEM
    whole = pl.BlockSpec(memory_space=pltpu.VMEM)
    wide = OWN + HALO
    forces, energies = pl.pallas_call(
        functools.partial(kernel, nx, ny),
        out_shape=(
            pltpu.VMEM((3, 2, 2, N), F32),
            pltpu.VMEM((HEADS, 2, 2, N), F32),
        ),
        in_specs=[pl.BlockSpec(memory_space=pl.ANY)] * 6,
        out_specs=(whole, whole),
        scratch_shapes=[
            vmem((4, 4, 8, N), F32),
            vmem((4, 3, N, N), F32),
            vmem((RADIAL * N, wide), BF16),
            vmem((RADIAL * N, wide), BF16),
            vmem((RADIAL * N, wide), BF16),
            vmem((RADIAL * N, wide), BF16),
            vmem((4, N, wide), F32),
            vmem((4, N, wide), F32),
            vmem((4, N, wide), F32),
            vmem((4, N, wide), F32),
            vmem((4, 4, RADIAL * SPECIES, N), F32),
            vmem((4, 4, N, CH + N), BF16),
            vmem((4, N, CH), F32),
            vmem((4, 4, N, CH), F32),
            vmem((4, N, CH), F32),
            vmem((4, RADIAL * N, CH + N), BF16),
            vmem((N, CH), BF16),
            vmem((64, CH), BF16),
            vmem((RADIAL, 1, CH), F32),
            vmem((N, CH), BF16),
            vmem((OWN, CH), BF16),
            vmem((4, N, N), BF16),
            vmem((4, N, CH), F32),
            vmem((OWN, CH), BF16),
            vmem((4, 4, 32, N), F32),
            vmem((8, 2, 32, N), F32),
            vmem((4, 32, N), F32),
            vmem((4, 3, N, N), F32),
            vmem((4, 4, 3, 8, N), F32),
            vmem((4, 4, 8, N), F32),
            vmem((8, 2, 8, N), F32),
            vmem((RADIAL * N, HALO), F32),
            vmem((RADIAL * N, HALO), F32),
            vmem((2, N, HALO), F32),
            vmem((2, N, HALO), F32),
            vmem((3, 2, 2, N), F32),
            vmem((2, 2, N), jnp.int32),
            vmem((2, 2, N), jnp.int32),
            vmem((RADIAL * SPECIES, CH), F32),
            vmem((RADIAL, CH), F32),
            vmem((HEADS, CH), BF16),
            pltpu.SemaphoreType.DMA((6,)),
            pltpu.SemaphoreType.DMA((4, 8)),
            pltpu.SemaphoreType.DMA((4, 8)),
        ],
        compiler_params=pltpu.CompilerParams(
            collective_id=0, has_side_effects=True, vmem_limit_bytes=56 * 1024 * 1024
        ),
    )(positions, valid_mask, species, density_table, radial_gain, readout.T)
    return forces, energies


def solution(mesh):
    nx, ny = mesh.shape["gx"], mesh.shape["gy"]
    in_specs = (P(None, "gx", "gy", None), P("gx", "gy", None), P("gx", "gy", None), P(), P(), P())
    out_specs = (P(None, "gx", "gy", None), P(None, "gx", "gy", None))
    return jax.shard_map(
        functools.partial(shards, nx, ny), mesh=mesh, in_specs=in_specs, out_specs=out_specs,
        check_vma=False,
    )
```

```python
import functools
import math

import jax
import jax.numpy as jnp
from jax import lax
from jax.experimental import pallas as pl
from jax.experimental.pallas import tpu as pltpu
from jax.sharding import PartitionSpec as P

MESH = pl.DeviceIdType.MESH
F32 = jnp.float32
BF16 = jnp.bfloat16

RADIAL = 8
SPECIES = 4
HEADS = 16
N = 128
CH = 256
CUT = 6.0
SOFT = 0.01
SPACE = CUT / (RADIAL - 1)
COEF = [math.exp(8.0 * k - k * k) for k in range(RADIAL)]
DIRS = [(-1, -1), (-1, 1), (1, -1), (1, 1), (-1, 0), (1, 0), (0, -1), (0, 1)]
OWN = 4 * N
HALO = 5 * N
ROWS = 32
BLOCKS = N // ROWS


def nn(a, b):
    return lax.dot_general(a, b, (((1,), (0,)), ((), ())), preferred_element_type=F32)


def tn(a, b):
    return lax.dot_general(a, b, (((0,), (0,)), ((), ())), preferred_element_type=F32)


def nt(a, b):
    return lax.dot_general(a, b, (((1,), (1,)), ((), ())), preferred_element_type=F32)


def border(d):
    return {1: 2, -1: 1, 0: pl.ds(1, 2)}[d]


def landing(d):
    return {1: 0, -1: 3, 0: pl.ds(1, 2)}[d]


def beyond(d):
    return {1: 3, -1: 0, 0: pl.ds(1, 2)}[d]


def own_slot(c):
    return 1 + c // 2, 1 + c % 2


def y_slots(c):
    return [(1, 3 * (c % 2)), (2, 3 * (c % 2))]


def x_slots(c):
    a = 3 * (c // 2)
    return [(a, 1), (a, 2), (a, 3 * (c % 2))]


def halo_slots(c):
    return y_slots(c) + x_slots(c)


GRAD_ORDER = ((0, (0,)), (1, (1, 4)), (2, (2, 6)), (3, (3, 5, 7)))
NEEDED = {2: (1, 4, 7), 3: (0, 6), 0: (3, 5), 1: (2,)}


PARTS = (
    (range(4), lambda c: [own_slot(j) for j in range(4)], 0, ()),
    (range(4), y_slots, OWN, (6, 7)),
    ((2, 3), x_slots, OWN + 2 * N, (4, 0, 1)),
    ((0, 1), lambda c: x_slots(c)[:2], OWN + 2 * N, (5,)),
    ((0, 1), lambda c: x_slots(c)[2:], OWN + 4 * N, (2, 3)),
)


def sigmoid(x):
    return 1.0 / (1.0 + jnp.exp(-x))


def kernel(
    nx, ny,
    pos_hbm, valid_hbm, spec_hbm, table_hbm, gain_hbm, readout_hbm,
    forces_ref, energies_ref,
    atoms, xi, basis_0, basis_1, basis_2, basis_3, u_s, a_s, rc_s, ri_s, dens, hid, hid_own, slope,
    msg, gms, tab_t, tab_s, gk, read_t, second, back_t, gm_own, gm_b,
    gpart, grecv, gsum, fi, fj, fpart, frecv, gs_a, gs_b, poly_s, slant_s,
    pos_ref, valid_ref, spec_ref, table_ref, gain_ref, readout_ref, load_sem,
    send_sem, recv_sem,
):
    gx, gy = lax.axis_index("gx"), lax.axis_index("gy")
    basis = (basis_0, basis_1, basis_2, basis_3)
    loads = [
        pltpu.make_async_copy(src, dst, load_sem.at[i])
        for i, (src, dst) in enumerate((
            (pos_hbm, pos_ref), (valid_hbm, valid_ref), (spec_hbm, spec_ref),
            (table_hbm, table_ref), (gain_hbm, gain_ref), (readout_hbm, readout_ref),
        ))
    ]
    for load in loads:
        load.start()
    own_slots = [own_slot(c) for c in range(4)]

    def turn(g):
        return jnp.where((g + 4) % 4 >= 2, -1, 1)

    side = turn(gx)
    own_row = {1: jnp.where(side > 0, 0, 1), 2: jnp.where(side > 0, 1, 0)}

    def peer(dx, dy):
        return (gx + side * dx, gy + dy)

    def there(dx, dy):
        ok = None
        for d, g, n in zip((dx, dy), peer(dx, dy), (nx, ny)):
            if d:
                one = jnp.logical_and(g >= 0, g < n)
                ok = one if ok is None else jnp.logical_and(ok, one)
        return ok

    def arrival(n):
        dx, dy = DIRS[n]
        if dx == 0:
            return landing(0), n
        up = jnp.where(side * turn(gx + side * dx) * dx > 0, 1, 0)
        return 3 - 3 * up, (2 * up + (1 if dy > 0 else 0) if dy else 4 + up)

    def copy(r, n, arrived, src, dst, device):
        return pltpu.make_async_remote_copy(
            src_ref=src, dst_ref=dst, send_sem=send_sem.at[r, n], recv_sem=recv_sem.at[r, arrived],
            device_id=device, device_id_type=MESH,
        )

    def exchange(r, wait, dirs, src_of, dst_of):
        for n in dirs:
            dx, dy = DIRS[n]
            if wait == "recv":
                @pl.when(there(-dx, -dy))
                def _():
                    dst = dst_of(dx, dy, landing(dx), n)
                    copy(r, n, n, src_of(dx, dy), dst, peer(-dx, -dy)).wait_recv()
            else:
                @pl.when(there(dx, dy))
                def _():
                    row, arrived = arrival(n)
                    dst = dst_of(dx, dy, row, arrived)
                    c = copy(r, n, arrived, src_of(dx, dy), dst, peer(dx, dy))
                    c.start() if wait == "start" else c.wait_send()

    def outward(r, buf, wait, dirs=range(8)):
        exchange(
            r, wait, dirs,
            lambda dx, dy: buf.at[border(dx), border(dy)],
            lambda dx, dy, row, n: buf.at[row, landing(dy)],
        )

    def inward(r, buf, land, wait, dirs=range(8)):
        exchange(
            r, wait, dirs,
            lambda dx, dy: buf.at[beyond(dx), beyond(dy)],
            lambda dx, dy, row, n: land.at[n, 0] if dx and dy else land.at[n],
        )

    def returned(land, a, b):
        total = None
        for n, (dx, dy) in enumerate(DIRS):
            if (dx == 0 or a == (1 if dx == 1 else 2)) and (dy == 0 or b == (1 if dy == 1 else 2)):
                m = a - 1 if dx == 0 else (b - 1 if dy == 0 else 0)
                total = land[n, m] if total is None else total + land[n, m]
        return total

    for a in range(4):
        for b in range(4):
            if not (a in (1, 2) and b in (1, 2)):
                atoms[a, b] = jnp.zeros((8, N), F32)
                dens[a, b] = jnp.zeros((RADIAL * SPECIES, N), F32)
    grecv[...] = jnp.zeros_like(grecv)
    frecv[...] = jnp.zeros_like(frecv)

    barrier = pltpu.get_barrier_semaphore()
    for dx, dy in DIRS:
        @pl.when(there(dx, dy))
        def _():
            pl.semaphore_signal(barrier, inc=1, device_id=peer(dx, dy), device_id_type=MESH)
    span_x = 1 + jnp.where(gx > 0, 1, 0) + jnp.where(gx < nx - 1, 1, 0)
    span_y = 1 + jnp.where(gy > 0, 1, 0) + jnp.where(gy < ny - 1, 1, 0)

    for load in loads:
        load.wait()
    for a, b in own_slots:
        rows = [pos_ref[i, own_row[a], b - 1 : b, :] for i in range(3)]
        rows.append(valid_ref[own_row[a], b - 1 : b, :].astype(F32))
        rows.append(spec_ref[own_row[a], b - 1 : b, :].astype(F32))
        rows.append(jnp.zeros((3, N), F32))
        atoms[a, b] = jnp.concatenate(rows, 0)

    table = table_ref[...] * 0.125
    high = table.astype(BF16).astype(F32)
    low = table - high
    tab_s[...] = jnp.concatenate([high, low], 0).astype(BF16)
    stacked = jnp.concatenate([high, high, low, jnp.zeros((32, CH), F32)], 0)
    tab_t[...] = stacked.astype(BF16)
    for k in range(RADIAL):
        row = gain_ref[k : k + 1, :] * (COEF[k] / 32.0)
        gk[k] = row
    read_t[...] = jnp.concatenate([readout_ref[...], jnp.zeros((N - HEADS, CH), BF16)], 0)
    for c in range(4):
        a, b = own_slot(c)
        tile = atoms[a, b]
        x = jnp.where(tile[3:4] > 0.0, tile[0:1], 1e4)
        xi[c, 0] = jnp.broadcast_to(x, (N, N)).T
        xi[c, 1] = jnp.broadcast_to(tile[1:2], (N, N)).T
        xi[c, 2] = jnp.broadcast_to(tile[2:3], (N, N)).T

    pl.semaphore_wait(barrier, span_x * span_y - 1)
    outward(0, atoms, "start")

    def offsets(c, rows, a, b):
        xj = jnp.where(atoms[a, b, 3:4, :] > 0.0, atoms[a, b, 0:1, :], -1e4)
        dx = xi[c, 0, rows, :] - xj
        dy = xi[c, 1, rows, :] - atoms[a, b, 1:2, :]
        dz = xi[c, 2, rows, :] - atoms[a, b, 2:3, :]
        return dx, dy, dz

    def pair_basis(c, block, a, b, lane, self_cell):
        rows = slice(block * ROWS, (block + 1) * ROWS)
        cols = slice(lane, lane + N)
        dx, dy, dz = offsets(c, rows, a, b)
        sq = dx * dx + dy * dy + (dz * dz + SOFT)
        if self_cell:
            i = lax.broadcasted_iota(jnp.int32, (ROWS, N), 0) + block * ROWS
            j = lax.broadcasted_iota(jnp.int32, (ROWS, N), 1)
            sq = jnp.where(i == j, 1e8, sq)
        ri = lax.rsqrt(sq)
        reach = jnp.maximum(1.0 - sq * (1.0 / (CUT * CUT)), 0.0)
        t = jnp.minimum(sq * ri * (1.0 / SPACE), float(RADIAL - 1))
        u = jnp.exp(2.0 * t - 8.0)
        amp = jnp.exp(-(t * t)) * reach
        u_s[c, rows, cols] = u
        a_s[c, rows, cols] = amp
        rc_s[c, rows, cols] = reach
        ri_s[c, rows, cols] = ri
        term = amp * reach
        for k in range(RADIAL):
            basis[c][k * N + block * ROWS : k * N + (block + 1) * ROWS, cols] = term.astype(BF16)
            if k < RADIAL - 1:
                term = term * u

    def part_pairs(c, part):
        _, slots_of, lane0, _ = PARTS[part]
        for block in range(BLOCKS):
            for m, (a, b) in enumerate(slots_of(c)):
                pair_basis(c, block, a, b, lane0 + m * N, part == 0 and m == c)

    def kinds(a, b, rows):
        kind = atoms[a, b, 4:5, :].astype(jnp.int32)
        r = lax.broadcasted_iota(jnp.int32, (rows, N), 0)
        return r, kind

    def selector(a, b):
        r, kind = kinds(a, b, N)
        hit = jnp.logical_and(r < 64, (r & 3) == kind)
        hid[a, b, :, CH:] = jnp.where(hit, 1.0, 0.0).T.astype(BF16)

    def hot(slots):
        parts = []
        for a, b in slots:
            r, kind = kinds(a, b, 16)
            parts.append(jnp.where(r == kind, 1.0, 0.0).astype(BF16))
        return jnp.concatenate(parts, 1)

    def part_density(c, part):
        _, slots_of, lane0, _ = PARTS[part]
        slots = slots_of(c)
        out = nt(hot(slots), basis[c][:, lane0 : lane0 + len(slots) * N])
        a, b = own_slots[c]
        for k in range(RADIAL):
            rows = slice(k * SPECIES, (k + 1) * SPECIES)
            piece = out[0:SPECIES, k * N : (k + 1) * N] * COEF[k]
            dens[a, b, rows, :] = dens[a, b, rows, :] + piece if part else piece

    last = None
    for part, (cells, slots_of, _, dirs) in enumerate(PARTS):
        outward(0, atoms, "recv", dirs)
        for c in cells:
            part_pairs(c, part)
            if last:
                part_density(*last)
            last = (c, part)
        if part == 2:
            part_density(*last)
            last = None
            outward(1, dens, "start", (5, 2, 3))
    part_density(*last)
    outward(1, dens, "start", (0, 1, 4, 6, 7))
    for a in range(4):
        for b in range(4):
            selector(a, b)

    def features(slots):
        parts = []
        for a, b in slots:
            d = dens[a, b]
            top = d.astype(BF16)
            rest = (d - top.astype(F32)).astype(BF16)
            parts.append(jnp.concatenate([top, rest, top, jnp.zeros((32, N), BF16)], 0))
        z = tn(jnp.concatenate(parts, 1), tab_t[...])
        s = sigmoid(z)
        h = z * s
        sp = s * (1.0 + z * (1.0 - s))
        for m, (a, b) in enumerate(slots):
            rows = slice(m * N, (m + 1) * N)
            hid[a, b, :, 0:CH] = h[rows].astype(BF16)
            slope[a, b] = sp[rows]
        return h

    h = features(own_slots)
    for c in range(4):
        hid_own[c] = h[c * N : (c + 1) * N]

    def gained(prod):
        total = prod[0:N] * gk[0]
        for k in range(1, RADIAL):
            total = total + prod[k * N : (k + 1) * N] * gk[k]
        return total

    def part_message(c, part):
        _, slots_of, lane0, _ = PARTS[part]
        slots = slots_of(c)
        h = jnp.concatenate([hid[a, b, :, 0:CH] for a, b in slots], 0)
        return gained(nn(basis[c][:, lane0 : lane0 + len(slots) * N], h))

    for c in range(4):
        msg[c] = part_message(c, 0) + hid_own[c]
    for part in (1, 2, 3, 4):
        cells, slots_of, _, dirs = PARTS[part]
        outward(1, dens, "recv", dirs)
        features(sorted({slot for c in cells for slot in slots_of(c)}))
        for c in cells:
            p = msg[c] + part_message(c, part)
            if part in (1, 3):
                msg[c] = p
                continue
            s = sigmoid(p)
            second[c * N : (c + 1) * N, :] = (p * s).astype(BF16)
            msg[c] = s * (1.0 + p * (1.0 - s))

    heads = nt(read_t[0:HEADS, :], second[...])
    sh = sigmoid(heads)
    valid = jnp.concatenate([atoms[a, b, 3:4, :] for a, b in own_slots], 1)
    out = valid * (heads * sh)
    back = (valid * (1.0 / HEADS)) * (sh * (1.0 + heads * (1.0 - sh)))
    for c, (a, b) in enumerate(own_slots):
        cols = slice(c * N, (c + 1) * N)
        for h in range(HEADS):
            energies_ref[h, own_row[a], b - 1 : b, :] = out[h : h + 1, cols]
        tile = jnp.concatenate([back[:, cols], jnp.zeros((N - HEADS, N), F32)], 0)
        back_t[c] = tile.T.astype(BF16)

    def project(x):
        out = nt(tab_s[...], x)
        return out[0:32] + out[32:64]

    def head_grad(c):
        dsec = nn(back_t[c], read_t[...]).astype(BF16).astype(F32)
        gm = dsec * msg[c]
        gm_own[c] = gm
        gm_b[c * N : (c + 1) * N, :] = gm.astype(BF16)
        for k in range(RADIAL):
            gms[c, k * N : (k + 1) * N, 0:CH] = (gm * gk[k]).astype(BF16)

    def halo_grad(c):
        x = tn(basis[c][:, OWN:], gms[c, :, 0:CH])
        slots = halo_slots(c)
        x = x * jnp.concatenate([slope[a, b] for a, b in slots], 0)
        out = project(x.astype(BF16))
        for m, (a, b) in enumerate(slots):
            gpart[a, b] += out[:, m * N : (m + 1) * N]

    gpart[...] = jnp.zeros_like(gpart)
    head_grad(0)
    for c, complete in GRAD_ORDER:
        if c < 3:
            head_grad(c + 1)
        halo_grad(c)
        inward(2, gpart, grecv, "start", complete)

    def own_grad(c):
        a, b = own_slots[c]
        x = gained(nn(basis[c][:, 0:OWN], gm_b[...])) + gm_own[c]
        gsum[c] = project((x * slope[a, b]).astype(BF16))

    upper, lower, both = slice(0, CH), slice(CH, CH + N), slice(0, CH + N)

    def gradients(c, slots, lanes, buf):
        h = jnp.concatenate([hid[a, b, :, lanes] for a, b in slots], 0)
        buf[:, 0 : h.shape[0]] = nt(gms[c, :, lanes], h)

    def horner(c, block, m, lane0, buf):
        rows = slice(block * ROWS, (block + 1) * ROWS)
        u = u_s[c, rows, lane0 + m * N : lane0 + (m + 1) * N]

        def grad(k):
            return buf[k * N + block * ROWS : k * N + (block + 1) * ROWS, m * N : (m + 1) * N]

        poly = grad(RADIAL - 1)
        slant = poly
        for k in range(RADIAL - 2, -1, -1):
            poly = poly * u + grad(k)
            if k:
                slant = slant * u + poly
        return poly, slant * u

    def second_layer_sums(c, buf):
        for block in range(BLOCKS):
            rows = slice(block * ROWS, (block + 1) * ROWS)
            for m in range(5):
                cols = slice(m * N, (m + 1) * N)
                poly_s[c, rows, cols], slant_s[c, rows, cols] = horner(c, block, m, OWN, buf)

    gradients(0, halo_slots(0), upper, gs_a)
    own_grad(0)
    second_layer_sums(0, gs_a)
    gradients(1, halo_slots(1), upper, gs_b)
    own_grad(1)
    second_layer_sums(1, gs_b)
    own_grad(2)
    own_grad(3)

    def density_grad(c):
        inward(2, gpart, grecv, "recv", NEEDED[c])
        a, b = own_slot(c)
        g = gsum[c] + returned(grecv, a, b)
        r = lax.broadcasted_iota(jnp.int32, (32, N), 0) >> 2
        coef = jnp.full((32, N), COEF[0], F32)
        for k in range(1, RADIAL):
            coef = jnp.where(r == k, COEF[k], coef)
        g = g * coef
        top = g.astype(BF16).astype(F32)
        gt = jnp.concatenate([top, g - top, jnp.zeros((64, N), F32)], 0).T
        lane = lax.broadcasted_iota(jnp.int32, (N, N), 1)
        for k in range(RADIAL):
            keep = jnp.logical_and(lane < 64, ((lane & 31) >> 2) == k)
            gms[c, k * N : (k + 1) * N, CH:] = jnp.where(keep, gt, 0.0).astype(BF16)

    fj[...] = jnp.zeros_like(fj)

    def block_forces(c, block, slots, lane0, buf):
        rows = slice(block * ROWS, (block + 1) * ROWS)
        sums = [jnp.zeros((ROWS, N), F32) for _ in range(3)]
        for m, (a, b) in enumerate(slots):
            cols = slice(lane0 + m * N, lane0 + (m + 1) * N)
            poly, slant = horner(c, block, m, lane0, buf)
            if lane0 and c < 2:
                halo = slice(m * N, (m + 1) * N)
                poly = poly + poly_s[c, rows, halo]
                slant = slant + slant_s[c, rows, halo]
            reach = rc_s[c, rows, cols]
            inner = ri_s[c, rows, cols] * slant * (2.0 / SPACE) - poly * (2.0 / SPACE**2)
            force = a_s[c, rows, cols] * (reach * inner - poly * (4.0 / CUT**2))
            for i, d in enumerate(offsets(c, rows, a, b)):
                f = force * d
                sums[i] = sums[i] + f
                part = f[0:8]
                for q in range(1, ROWS // 8):
                    part = part + f[8 * q : 8 * q + 8]
                fj[a, b, i] += part
        for i in range(3):
            if lane0:
                fi[c, i, rows, :] = sums[i]
            else:
                fi[c, i, rows, :] += sums[i]

    def halo_forces(c, buf):
        for block in range(BLOCKS):
            block_forces(c, block, halo_slots(c), OWN, buf)

    def own_forces(c, buf):
        for block in range(BLOCKS):
            block_forces(c, block, own_slots, 0, buf)

    def halo_force(n):
        dx, dy = DIRS[n]
        for a in {1: (3,), -1: (0,), 0: (1, 2)}[dx]:
            for b in {1: (3,), -1: (0,), 0: (1, 2)}[dy]:
                rows = [jnp.sum(fj[a, b, i], 0, keepdims=True) for i in range(3)]
                fpart[a, b] = jnp.concatenate(rows + [jnp.zeros((5, N), F32)], 0)

    def send_forces(dirs):
        for n in dirs:
            halo_force(n)
        inward(3, fpart, frecv, "start", dirs)

    density_grad(2)
    gradients(2, halo_slots(2), both, gs_a)
    density_grad(3)
    halo_forces(2, gs_a)
    gradients(3, halo_slots(3), both, gs_b)
    send_forces((2,))
    halo_forces(3, gs_b)
    send_forces((3, 5))
    density_grad(0)
    gradients(0, halo_slots(0), lower, gs_a)
    density_grad(1)
    halo_forces(0, gs_a)
    gradients(1, halo_slots(1), lower, gs_b)
    send_forces((0, 6))
    halo_forces(1, gs_b)
    gradients(0, own_slots, both, gs_a)
    send_forces((1, 4, 7))
    own_forces(0, gs_a)
    gradients(1, own_slots, both, gs_b)
    own_forces(1, gs_b)
    gradients(2, own_slots, both, gs_a)
    own_forces(2, gs_a)
    gradients(3, own_slots, both, gs_b)
    own_forces(3, gs_b)
    sums = []
    for c in range(4):
        a, b = own_slot(c)
        rows = []
        for i in range(3):
            mine = jnp.sum(fi[c, i].T, 0, keepdims=True)
            rows.append(jnp.sum(fj[a, b, i], 0, keepdims=True) - mine)
        sums.append(jnp.concatenate(rows + [jnp.zeros((5, N), F32)], 0))
    outward(0, atoms, "send")
    outward(1, dens, "send")
    inward(2, gpart, grecv, "send")
    inward(3, fpart, frecv, "send")
    inward(3, fpart, frecv, "recv")
    for c in range(4):
        a, b = own_slot(c)
        total = sums[c] + returned(frecv, a, b)
        for i in range(3):
            forces_ref[i, own_row[a], b - 1 : b, :] = total[i : i + 1]


def shards(nx, ny, positions, valid_mask, species, density_table, radial_gain, readout):
    vmem = pltpu.VMEM
    whole = pl.BlockSpec(memory_space=pltpu.VMEM)
    wide = OWN + HALO
    forces, energies = pl.pallas_call(
        functools.partial(kernel, nx, ny),
        out_shape=(
            pltpu.VMEM((3, 2, 2, N), F32),
            pltpu.VMEM((HEADS, 2, 2, N), F32),
        ),
        in_specs=[pl.BlockSpec(memory_space=pl.ANY)] * 6,
        out_specs=(whole, whole),
        scratch_shapes=[
            vmem((4, 4, 8, N), F32),
            vmem((4, 3, N, N), F32),
            vmem((RADIAL * N, wide), BF16),
            vmem((RADIAL * N, wide), BF16),
            vmem((RADIAL * N, wide), BF16),
            vmem((RADIAL * N, wide), BF16),
            vmem((4, N, wide), F32),
            vmem((4, N, wide), F32),
            vmem((4, N, wide), F32),
            vmem((4, N, wide), F32),
            vmem((4, 4, RADIAL * SPECIES, N), F32),
            vmem((4, 4, N, CH + N), BF16),
            vmem((4, N, CH), F32),
            vmem((4, 4, N, CH), F32),
            vmem((4, N, CH), F32),
            vmem((4, RADIAL * N, CH + N), BF16),
            vmem((N, CH), BF16),
            vmem((64, CH), BF16),
            vmem((RADIAL, 1, CH), F32),
            vmem((N, CH), BF16),
            vmem((OWN, CH), BF16),
            vmem((4, N, N), BF16),
            vmem((4, N, CH), F32),
            vmem((OWN, CH), BF16),
            vmem((4, 4, 32, N), F32),
            vmem((8, 2, 32, N), F32),
            vmem((4, 32, N), F32),
            vmem((4, 3, N, N), F32),
            vmem((4, 4, 3, 8, N), F32),
            vmem((4, 4, 8, N), F32),
            vmem((8, 2, 8, N), F32),
            vmem((RADIAL * N, HALO), F32),
            vmem((RADIAL * N, HALO), F32),
            vmem((2, N, HALO), F32),
            vmem((2, N, HALO), F32),
            vmem((3, 2, 2, N), F32),
            vmem((2, 2, N), jnp.int32),
            vmem((2, 2, N), jnp.int32),
            vmem((RADIAL * SPECIES, CH), F32),
            vmem((RADIAL, CH), F32),
            vmem((HEADS, CH), BF16),
            pltpu.SemaphoreType.DMA((6,)),
            pltpu.SemaphoreType.DMA((4, 8)),
            pltpu.SemaphoreType.DMA((4, 8)),
        ],
        compiler_params=pltpu.CompilerParams(
            collective_id=0, has_side_effects=True, vmem_limit_bytes=56 * 1024 * 1024
        ),
    )(positions, valid_mask, species, density_table, radial_gain, readout.T)
    return forces, energies


def solution(mesh):
    nx, ny = mesh.shape["gx"], mesh.shape["gy"]
    in_specs = (P(None, "gx", "gy", None), P("gx", "gy", None), P("gx", "gy", None), P(), P(), P())
    out_specs = (P(None, "gx", "gy", None), P(None, "gx", "gy", None))
    return jax.shard_map(
        functools.partial(shards, nx, ny), mesh=mesh, in_specs=in_specs, out_specs=out_specs,
        check_vma=False,
    )
```
